256 devices in a mesh: pair: 16 (over x_lo, z), tm: 8 (over y, core), band: 2 (over x_hi).
Axes of the slice: x: 4 (x_hi: 2, x_lo: 2; x = x_hi * 2 + x_lo), y: 4, z: 8, core: 2. Of those that a mesh axis runs over, the one named last changes fastest.
Arguments:
- spectra: bfloat16 [2, 64, 1024, 1024], P(None, 'tm', 'pair', 'band'), may hold values from -200 to 200
- quality: int32 [64, 1024], P('tm', 'pair'), may hold values 0 or 1
Outputs:
- xcorr: bfloat16 [16, 2, 9, 2, 512, 4096], P('pair', None, None, 'band', 'tm')
The draws below stay inside these ranges and needn't reach their ends.
All inputs are finite; a program needn't handle non-finite values. No bound on the sum of `quality` on one device may be relied on, other than what follows from the above.
Results may differ from the reference program's by a relative error of at most 0.0056.
Values may be sent and summed in bfloat16 or wider, within the bound.
A program may use at most 128 MiB of HBM per device.

```python
import jax
import jax.numpy as jnp
from jax import lax

CB = 64
BINS = 1024
SMOOTH = 32
WINDOWS = 64
BLOCKS = 16
CHANNELS = 1024
STEPS = 9
BANDS = 2
BAND_BINS = 512


def draw_spectra(key, part):
    key = jax.random.fold_in(key, 11)
    key_base, key_level, key_profile = jax.random.split(key, 3)
    full_shape = (2, WINDOWS, CHANNELS, BINS)
    noise_part = jnp.clip(jax.random.normal(key_base, full_shape, jnp.float32), -6.0, 6.0)
    channel_level = 10.0 ** jax.random.uniform(key_level, (1, WINDOWS, CHANNELS, 1), jnp.float32, 0.0, 1.0)
    profile = 10.0 ** jax.random.uniform(key_profile, (1, 1, 1, BINS), jnp.float32, -0.5, 0.5)
    return (noise_part * channel_level * profile).astype(jnp.bfloat16)


def with_ends(values, rng, low, largest):
    index_at = [jax.random.randint(jax.random.fold_in(rng, axis), (), 0, length) for axis, length in enumerate(values.shape)]
    longest = values.shape.index(max(values.shape))
    beside = index_at[:longest] + [(index_at[longest] + 1) % values.shape[longest]] + index_at[longest + 1:]
    return values.at[tuple(index_at)].set(low).at[tuple(beside)].set(largest)


def setup_inputs(seed: int = 0) -> dict:
    splits = jax.random.split(jax.random.key(seed), 3)
    spectra = draw_spectra(jax.random.fold_in(splits[2], 71), 0)
    quality = with_ends((jax.random.randint(splits[1], (WINDOWS, CHANNELS), 0, 8) < 7).astype(jnp.int32), jax.random.fold_in(splits[1], 1), 0, 1)
    return {"spectra": spectra, "quality": quality}


def whiten(block, kept_mask):
    real_imag = block.astype(jnp.float32)
    power_sum = real_imag[0] * real_imag[0] + real_imag[1] * real_imag[1]
    padded = jnp.pad(power_sum, ((0, 0), (0, 0), (SMOOTH, SMOOTH)))
    smooth = lax.reduce_window(padded, jnp.array(0.0, power_sum.dtype), lax.add, (1, 1, 2 * SMOOTH + 1), (1, 1, 1), 'VALID')
    scaling = lax.rsqrt(smooth / (2 * SMOOTH + 1) + 1e-06) * kept_mask.astype(jnp.float32)[:, :, None]
    return (real_imag * scaling[None]).astype(jnp.bfloat16)

def reference(spectra, quality):
    blocks = spectra.reshape(2, WINDOWS, BLOCKS, CB, BINS).transpose(2, 0, 1, 3, 4)
    masks = quality.reshape(WINDOWS, BLOCKS, CB).transpose(1, 0, 2)
    whitened = lax.map(lambda pair_args: whiten(pair_args[0], pair_args[1]), (blocks, masks))
    stack_norm = 1.0 / WINDOWS ** 0.5

    def one_block(block_index):
        own_block = whitened[block_index].astype(jnp.float32)
        flipped = jnp.stack((own_block[1], -own_block[0]))
        left_pair = jnp.stack((own_block, flipped))
        per_step = []
        for offset in range(STEPS):
            other_block = whitened[(block_index - offset) % BLOCKS].astype(jnp.float32)
            product = jnp.einsum('kcwib,cwjb->kbij', left_pair, other_block) * stack_norm
            per_step.append(product.reshape(2, BANDS, BAND_BINS, CB * CB))
        return jnp.stack(per_step, 1).astype(jnp.bfloat16)
    return lax.map(one_block, jnp.arange(BLOCKS, dtype=jnp.int32))
```

```python
import jax
import jax.numpy as jnp
from jax import lax
from jax.experimental import pallas as pl
from jax.experimental.pallas import tpu as pltpu
from jax.sharding import PartitionSpec as P

MESH = pl.DeviceIdType.MESH
SMOOTH = 32
WIDTH = 2 * SMOOTH + 1
WIN = 8
CB = 64
BAND = 512
PIECES = 8
FLO = 32
STEPS = 9
F32 = jnp.float32
BF16 = jnp.bfloat16


def iota(shape, dim):
    return lax.broadcasted_iota(jnp.int32, shape, dim)


def kernel(
    spec, quality, out,
    X, LHS, O, stage, SC, PH, PL, BM, W, T, halo_out, halo_in,
    halo_sem, a2a_send, recv, send, out_sem,
):
    p = lax.axis_index("pair")
    t = lax.axis_index("tm")
    band = lax.axis_index("band")
    y, core = t // 2, t % 2
    nxt, prv, opp = (p + 1) % 16, (p + 15) % 16, (p + 8) % 16

    barrier = pltpu.get_barrier_semaphore()
    for target in (nxt, prv, opp):
        pl.semaphore_signal(barrier, inc=1, device_id={"pair": target}, device_id_type=MESH)
    for step in range(1, 8):
        pl.semaphore_signal(barrier, inc=1, device_id={"tm": (t + step) % 8}, device_id_type=MESH)
    pl.semaphore_signal(barrier, inc=1, device_id={"band": 1 - band}, device_id_type=MESH)

    def power(w, lanes):
        re = spec[0, w, :, lanes].astype(F32)
        im = spec[1, w, :, lanes].astype(F32)
        return re * re + im * im

    group = iota((16, 128), 1) // 32
    for w in range(WIN):
        last = pltpu.roll(power(w, slice(BAND - 128, BAND)), 32, 1)
        first = power(w, slice(0, 128))
        edge = jnp.where(band == 0, last, first)
        packed = edge[0:16]
        for g in range(1, 4):
            packed = jnp.where(group == g, pltpu.roll(edge[16 * g : 16 * g + 16], 32 * g, 1), packed)
        halo_out[w * 16 : w * 16 + 16, :] = packed.astype(BF16)

    pl.semaphore_wait(barrier, 11)
    halo = pltpu.make_async_remote_copy(
        src_ref=halo_out, dst_ref=halo_in, send_sem=halo_sem.at[0], recv_sem=halo_sem.at[1],
        device_id={"band": 1 - band}, device_id_type=MESH,
    )
    halo.start()

    BM[...] = jnp.where(jnp.abs(iota((BAND, BAND), 0) - iota((BAND, BAND), 1)) <= SMOOTH, 1.0, 0.0).astype(BF16)

    def split(w, c):
        pw = power(w, slice(None))
        hi = pw.astype(BF16)
        rows = pl.ds(pl.multiple_of(w * CB, CB), CB)
        PH[rows, :] = hi
        PL[rows, :] = (pw - hi.astype(F32)).astype(BF16)
        return c

    lax.fori_loop(0, WIN, split, 0)

    def smooth(m, c):
        rows = pl.ds(pl.multiple_of(m * 128, 128), 128)
        total = jnp.dot(PH[rows, :], BM[...], preferred_element_type=F32)
        total += jnp.dot(PL[rows, :], BM[...], preferred_element_type=F32)
        for tile in range(4):
            SC[tile, rows, :] = total[:, tile * 128 : tile * 128 + 128]
        return c

    lax.fori_loop(0, WIN * CB // 128, smooth, 0)

    halo.wait_recv()
    src, dst = iota((128, BAND), 0), iota((128, BAND), 1)
    l, e = src % 32, dst % 128
    near = jnp.where(band == 0, e - 96 - l, l - e) >= 0
    hb = jnp.where((src // 32 == dst // 128) & near, 1.0, 0.0).astype(BF16)
    extra = jnp.dot(halo_in[...], hb, preferred_element_type=F32)
    eye = iota((CB, CB), 0) == iota((CB, CB), 1)
    for w in range(WIN):
        more = jnp.concatenate([extra[w * 16 : w * 16 + 16, g * 128 : g * 128 + 128] for g in range(4)], axis=0)
        q = quality[w : w + 1, :].astype(F32)
        column = jnp.sum(jnp.where(eye, q, 0.0), axis=1, keepdims=True)
        for tile in range(4):
            rows = slice(w * CB, w * CB + CB)
            total = SC[tile, rows, :]
            if tile == 0:
                total = total + jnp.where(band == 1, more, 0.0)
            if tile == 3:
                total = total + jnp.where(band == 0, more, 0.0)
            SC[tile, rows, :] = lax.rsqrt(total * (1.0 / WIDTH) + 1e-06) * column

    def a2a_copy(o, dc):
        dy = o ^ (o >> 1)
        target = ((y + dy) % 4) * 2 + (core ^ dc)
        n = 2 * o + dc
        return pltpu.make_async_remote_copy(
            src_ref=X.at[72 + n], dst_ref=X.at[n], send_sem=a2a_send.at[n], recv_sem=recv.at[0, n],
            device_id={"tm": target}, device_id_type=MESH,
        )

    low = iota((CB, 128), 1) % 64 < 32

    def whiten(o, c):
        dy = o ^ (o >> 1)
        tile = (y + dy) % 4
        lanes = pl.ds(pl.multiple_of(tile * 128, 128), 128)
        for w in range(WIN):
            scale = SC[tile, w * CB : w * CB + CB, :]
            re = spec[0, w, :, lanes].astype(F32) * scale
            im = spec[1, w, :, lanes].astype(F32) * scale
            top = jnp.where(low, re, pltpu.roll(im, 32, 1))
            bottom = jnp.where(low, pltpu.roll(re, 96, 1), im)
            turned = jnp.concatenate([top, bottom], axis=0).T
            for half in range(2):
                for k in range(2):
                    at = half * 64 + k * 32
                    W[pl.ds(half * 512 + k * 8 + w, FLO, stride=16), :] = turned[at : at + 32]
        for half in range(2):
            dc = half ^ core
            piece = jnp.where((o == 0) & (dc == 0), 0, 72 + 2 * o + dc)
            X[piece] = W[half * 512 : half * 512 + 512, :].astype(BF16).reshape(FLO, 16, 128)

        @pl.when(o > 0)
        def _():
            a2a_copy(o, 0).start()

        a2a_copy(o, 1).start()
        return c

    lax.fori_loop(0, 4, whiten, 0)

    def hop(src_slot, dst_slot, n, count, target, row, sem, recv_at):
        return pltpu.make_async_remote_copy(
            src_ref=X.at[pl.ds(src_slot * 8 + n, count)], dst_ref=X.at[pl.ds(dst_slot * 8 + n, count)],
            send_sem=send.at[row, sem], recv_sem=recv.at[dst_slot, recv_at],
            device_id={"pair": target}, device_id_type=MESH,
        )

    def first_forward(n):
        return hop(0, 1, n, 1, nxt, 0, n, n)

    def exchange(n):
        return hop(0, 8, n, 1, opp, 1, n, n)

    def first_back(n):
        return hop(8, 7, n, 1, prv, 2, n, n)

    LAG = 2

    def early(n, c):
        @pl.when((n >= 1) & (n < 8))
        def _():
            a2a_copy(n // 2, n % 2).wait_recv()

        @pl.when(n < 8)
        def _():
            first_forward(n).start()
            exchange(n).start()

        @pl.when(n >= LAG)
        def _():
            exchange(n - LAG).wait_recv()
            first_back(n - LAG).start()

        return c

    lax.fori_loop(0, 8 + LAG, early, 0)

    def pieces_in(copy, start):
        def one(n, c):
            copy(n).wait_recv()
            return c

        lax.fori_loop(start, start + 4, one, 0)

    def forward(slot, half):
        return hop(slot, slot + 1, 4 * half, 4, nxt, 2 + slot, half, half)

    def back(slot, half):
        return hop(slot, slot - 1, 4 * half, 4, prv, 13 - slot, half, half)

    lane = iota((CB // 2, 128), 1)

    def prepare(fp, c):
        x = X[0:8, fp].reshape(128, 128).astype(F32)
        T[...] = x.T
        for hi in range(2):
            for odd in range(2):
                a = T[pl.ds(hi * 64 + odd, 32, stride=2), :]
                b = jnp.where(lane % 16 < 8, pltpu.roll(a, 120, 1), -pltpu.roll(a, 8, 1))
                LHS[hi * FLO + fp, 0:32, odd * 128 : odd * 128 + 128] = a.astype(BF16)
                LHS[hi * FLO + fp, 32:64, odd * 128 : odd * 128 + 128] = b.astype(BF16)
        return c

    low64 = iota((128, 128), 1) < 64

    def out_copy(slot, buf, k):
        return pltpu.make_async_copy(stage.at[buf, k], out.at[k, slot], out_sem.at[buf, k])

    def correlate(slot, buf, wait_slot):
        def one(fp, c):
            x = X[pl.ds(slot * 8, 8), fp].reshape(128, 128).astype(F32)
            rolled = pltpu.roll(x, 64, 1)
            zero = jnp.zeros_like(x)
            r0 = jnp.concatenate([jnp.where(low64, x, zero), jnp.where(low64, zero, rolled)], axis=0).astype(BF16)
            r1 = jnp.concatenate([jnp.where(low64, rolled, zero), jnp.where(low64, zero, x)], axis=0).astype(BF16)
            for hi, r in ((0, r0), (1, r1)):
                f = hi * FLO + fp
                O[pl.ds(f, 64, stride=64), :] = jnp.dot(LHS[f], r, preferred_element_type=F32)
            return c

        lax.fori_loop(0, FLO, one, 0)
        if wait_slot is not None:
            for k in range(2):
                out_copy(wait_slot, buf, k).wait()
        for k in range(2):
            for i in range(32):
                at = (k * 32 + i) * 64
                stage[buf, k, :, i * 128 : i * 128 + 128] = (O[at : at + 64, :] * 0.125).astype(BF16)
            out_copy(slot, buf, k).start()

    pieces_in(first_forward, 0)
    forward(1, 0).start()
    pieces_in(first_back, 0)
    back(7, 0).start()
    lax.fori_loop(0, FLO, prepare, 0)
    correlate(0, 0, None)
    pieces_in(first_forward, 4)
    forward(1, 1).start()
    pieces_in(first_back, 4)
    back(7, 1).start()
    correlate(8, 1, None)
    correlate(1, 0, 0)
    correlate(7, 1, 8)
    forward(1, 0).wait_recv()
    forward(2, 0).start()
    back(7, 0).wait_recv()
    back(7, 1).wait_recv()
    back(6, 1).start()
    back(6, 0).start()
    forward(1, 1).wait_recv()
    forward(2, 1).start()
    correlate(2, 0, 1)
    correlate(6, 1, 7)
    forward(2, 0).wait_recv()
    forward(3, 0).start()
    back(6, 1).wait_recv()
    back(5, 1).start()
    forward(2, 1).wait_recv()
    correlate(3, 0, 2)
    back(6, 0).wait_recv()
    correlate(5, 1, 6)
    forward(3, 0).wait_recv()
    back(5, 1).wait_recv()
    correlate(4, 0, 3)

    for k in range(2):
        out_copy(5, 1, k).wait()
        out_copy(4, 0, k).wait()
    halo.wait_send()

    def sent(n, c):
        @pl.when(n > 0)
        def _():
            a2a_copy(n // 2, n % 2).wait_send()

        first_forward(n).wait_send()
        exchange(n).wait_send()
        first_back(n).wait_send()
        return c

    lax.fori_loop(0, 8, sent, 0)
    for half in range(2):
        for slot in (1, 2):
            forward(slot, half).wait_send()
        for slot in (7, 6):
            back(slot, half).wait_send()
    forward(3, 0).wait_send()
    back(5, 1).wait_send()


def body(spectra, quality):
    result = pl.pallas_call(
        kernel,
        out_shape=jax.ShapeDtypeStruct((2, STEPS, 64, CB * CB), BF16),
        in_specs=[pl.BlockSpec(memory_space=pltpu.VMEM)] * 2,
        out_specs=pl.BlockSpec(memory_space=pl.ANY),
        scratch_shapes=[
            pltpu.VMEM((80, FLO, 16, 128), BF16),
            pltpu.VMEM((64, 64, 256), BF16),
            pltpu.VMEM((64 * 64, 128), F32),
            pltpu.VMEM((2, 2, 64, CB * CB), BF16),
            pltpu.VMEM((4, WIN * CB, 128), F32),
            pltpu.VMEM((WIN * CB, BAND), BF16),
            pltpu.VMEM((WIN * CB, BAND), BF16),
            pltpu.VMEM((BAND, BAND), BF16),
            pltpu.VMEM((1024, 128), F32),
            pltpu.VMEM((128, 128), F32),
            pltpu.VMEM((128, 128), BF16),
            pltpu.VMEM((128, 128), BF16),
            pltpu.SemaphoreType.DMA((2,)),
            pltpu.SemaphoreType.DMA((8,)),
            pltpu.SemaphoreType.DMA((9, 8)),
            pltpu.SemaphoreType.DMA((9, 8)),
            pltpu.SemaphoreType.DMA((2, 2)),
        ],
        compiler_params=pltpu.CompilerParams(
            collective_id=0, has_side_effects=True, vmem_limit_bytes=40 * 1024 * 1024
        ),
        cost_estimate=pl.CostEstimate(flops=1300000000, bytes_accessed=11000000, transcendentals=262144),
    )(spectra, quality)
    return result.reshape(1, 2, STEPS, 1, 64, CB * CB)


def solution(mesh):
    return jax.shard_map(
        body,
        mesh=mesh,
        in_specs=(P(None, "tm", "pair", "band"), P("tm", "pair")),
        out_specs=P("pair", None, None, "band", "tm", None),
        check_vma=False,
    )
```

```python
import jax
import jax.numpy as jnp
from jax import lax
from jax.experimental import pallas as pl
from jax.experimental.pallas import tpu as pltpu
from jax.sharding import PartitionSpec as P

MESH = pl.DeviceIdType.MESH
SMOOTH = 32
WIDTH = 2 * SMOOTH + 1
WIN = 8
CB = 64
BAND = 512
PIECES = 8
FLO = 32
STEPS = 9
UNROLL = 8
PAD = 72
F32 = jnp.float32
BF16 = jnp.bfloat16


def iota(shape, dim):
    return lax.broadcasted_iota(jnp.int32, shape, dim)


def kernel(
    spec_in, quality_in, out,
    spec, quality, X, LHS, O, SC, PH, PL, BM, W, T, halo_out, halo_in,
    in_sem, halo_sem, a2a_send, recv, send,
):
    p = lax.axis_index("pair")
    t = lax.axis_index("tm")
    band = lax.axis_index("band")
    y, core = t // 2, t % 2
    nxt, prv, opp = (p + 1) % 16, (p + 15) % 16, (p + 8) % 16
    z = p % 8
    wrap = z % 7 == 0
    far = p - z + 7 - z
    load_spec = pltpu.make_async_copy(spec_in, spec, in_sem.at[0])
    load_quality = pltpu.make_async_copy(quality_in, quality, in_sem.at[1])
    load_spec.start()
    load_quality.start()

    barrier = pltpu.get_barrier_semaphore()
    for target in (nxt, prv, opp):
        pl.semaphore_signal(barrier, inc=1, device_id={"pair": target}, device_id_type=MESH)
    for step in range(1, 8):
        pl.semaphore_signal(barrier, inc=1, device_id={"tm": (t + step) % 8}, device_id_type=MESH)
    pl.semaphore_signal(barrier, inc=1, device_id={"band": 1 - band}, device_id_type=MESH)

    @pl.when(wrap)
    def _():
        pl.semaphore_signal(barrier, inc=1, device_id={"pair": far}, device_id_type=MESH)

    load_spec.wait()
    load_quality.wait()

    def power(w, lanes):
        re = spec[0, w, :, lanes].astype(F32)
        im = spec[1, w, :, lanes].astype(F32)
        return re * re + im * im

    group = iota((16, 128), 1) // 32
    for w in range(WIN):
        last = pltpu.roll(power(w, slice(BAND - 128, BAND)), 32, 1)
        first = power(w, slice(0, 128))
        edge = jnp.where(band == 0, last, first)
        packed = edge[0:16]
        for g in range(1, 4):
            packed = jnp.where(group == g, pltpu.roll(edge[16 * g : 16 * g + 16], 32 * g, 1), packed)
        halo_out[w * 16 : w * 16 + 16, :] = packed.astype(BF16)

    pl.semaphore_wait(barrier, jnp.where(wrap, 12, 11))
    halo = pltpu.make_async_remote_copy(
        src_ref=halo_out, dst_ref=halo_in, send_sem=halo_sem.at[0], recv_sem=halo_sem.at[1],
        device_id={"band": 1 - band}, device_id_type=MESH,
    )
    halo.start()

    BM[...] = jnp.where(jnp.abs(iota((BAND, BAND), 0) - iota((BAND, BAND), 1)) <= SMOOTH, 1.0, 0.0).astype(BF16)

    def split(w, c):
        pw = power(w, slice(None))
        hi = pw.astype(BF16)
        rows = pl.ds(pl.multiple_of(w * CB, CB), CB)
        PH[rows, :] = hi
        PL[rows, :] = (pw - hi.astype(F32)).astype(BF16)
        return c

    lax.fori_loop(0, WIN, split, 0)

    def smooth(m, c):
        rows = pl.ds(pl.multiple_of(m * 128, 128), 128)
        total = jnp.dot(PH[rows, :], BM[...], preferred_element_type=F32)
        total += jnp.dot(PL[rows, :], BM[...], preferred_element_type=F32)
        for tile in range(4):
            SC[tile, rows, :] = total[:, tile * 128 : tile * 128 + 128]
        return c

    lax.fori_loop(0, WIN * CB // 128, smooth, 0)

    halo.wait_recv()
    src, dst = iota((128, BAND), 0), iota((128, BAND), 1)
    l, e = src % 32, dst % 128
    near = jnp.where(band == 0, e - 96 - l, l - e) >= 0
    hb = jnp.where((src // 32 == dst // 128) & near, 1.0, 0.0).astype(BF16)
    extra = jnp.dot(halo_in[...], hb, preferred_element_type=F32)
    eye = iota((CB, CB), 0) == iota((CB, CB), 1)
    for w in range(WIN):
        more = jnp.concatenate([extra[w * 16 : w * 16 + 16, g * 128 : g * 128 + 128] for g in range(4)], axis=0)
        q = quality[w : w + 1, :].astype(F32)
        column = jnp.sum(jnp.where(eye, q, 0.0), axis=1, keepdims=True)
        for tile in range(4):
            rows = slice(w * CB, w * CB + CB)
            total = SC[tile, rows, :]
            if tile == 0:
                total = total + jnp.where(band == 1, more, 0.0)
            if tile == 3:
                total = total + jnp.where(band == 0, more, 0.0)
            SC[tile, rows, :] = lax.rsqrt(total * (1.0 / WIDTH) + 1e-06) * column

    def a2a_copy(o, dc):
        dy = o ^ (o >> 1)
        target = ((y + dy) % 4) * 2 + (core ^ dc)
        n = 2 * o + dc
        return pltpu.make_async_remote_copy(
            src_ref=X.at[72 + n], dst_ref=X.at[n], send_sem=a2a_send.at[n], recv_sem=recv.at[0, n],
            device_id={"tm": target}, device_id_type=MESH,
        )

    low = iota((CB, 128), 1) % 64 < 32

    def whiten(o, c):
        dy = o ^ (o >> 1)
        tile = (y + dy) % 4
        lanes = pl.ds(pl.multiple_of(tile * 128, 128), 128)
        for w in range(WIN):
            scale = SC[tile, w * CB : w * CB + CB, :]
            re = spec[0, w, :, lanes].astype(F32) * scale
            im = spec[1, w, :, lanes].astype(F32) * scale
            top = jnp.where(low, re, pltpu.roll(im, 32, 1))
            bottom = jnp.where(low, pltpu.roll(re, 96, 1), im)
            turned = jnp.concatenate([top, bottom], axis=0).T
            for half in range(2):
                for k in range(2):
                    at = half * 64 + k * 32
                    W[pl.ds(half * 512 + k * 8 + w, FLO, stride=16), :] = turned[at : at + 32]
        for half in range(2):
            dc = half ^ core
            piece = jnp.where((o == 0) & (dc == 0), 0, 72 + 2 * o + dc)
            X[piece] = W[half * 512 : half * 512 + 512, :].astype(BF16).reshape(FLO, 16, 128)

        @pl.when(o > 0)
        def _():
            a2a_copy(o, 0).start()

        a2a_copy(o, 1).start()
        return c

    lax.fori_loop(0, 4, whiten, 0)

    def hop(src_slot, dst_slot, n, count, target, row, sem, recv_at):
        return pltpu.make_async_remote_copy(
            src_ref=X.at[pl.ds(src_slot * 8 + n, count)], dst_ref=X.at[pl.ds(dst_slot * 8 + n, count)],
            send_sem=send.at[row, sem], recv_sem=recv.at[dst_slot, recv_at],
            device_id={"pair": target}, device_id_type=MESH,
        )

    def first_forward(n):
        return hop(jnp.where(z == 7, 8, 0), 1, n, 1, jnp.where(z == 7, far, nxt), 0, n, n)

    def exchange(n):
        return hop(0, 8, n, 1, opp, 1, n, n)

    def first_back(n):
        return hop(jnp.where(z == 0, 0, 8), 7, n, 1, jnp.where(z == 0, far, prv), 2, n, n)

    LAG = 2

    def early(n, c):
        @pl.when((n >= 1) & (n < 8))
        def _():
            a2a_copy(n // 2, n % 2).wait_recv()

        @pl.when(n < 8)
        def _():
            exchange(n).start()

        @pl.when((n < 8) & (z != 7))
        def _():
            first_forward(n).start()

        @pl.when((n < 8) & (z == 0))
        def _():
            first_back(n).start()

        @pl.when(n >= LAG)
        def _():
            exchange(n - LAG).wait_recv()

        @pl.when((n >= LAG) & (z == 7))
        def _():
            first_forward(n - LAG).start()

        @pl.when((n >= LAG) & (z != 0))
        def _():
            first_back(n - LAG).start()

        return c

    lax.fori_loop(0, 8 + LAG, early, 0)

    def pieces_in(copy, start):
        def one(n, c):
            copy(n).wait_recv()
            return c

        lax.fori_loop(start, start + 4, one, 0)

    def forward(slot, half):
        return hop(slot, slot + 1, 4 * half, 4, nxt, 2 + slot, half, half)

    def back(slot, half):
        return hop(slot, slot - 1, 4 * half, 4, prv, 13 - slot, half, half)

    lane = iota((CB // 2, 128), 1)

    def prepare(fp, c):
        x = X[0:8, fp].reshape(128, 128).astype(F32)
        T[...] = x.T
        for hi in range(2):
            for odd in range(2):
                a = T[pl.ds(hi * 64 + odd, 32, stride=2), :]
                b = jnp.where(lane % 16 < 8, pltpu.roll(a, 120, 1), -pltpu.roll(a, 8, 1))
                LHS[hi * FLO + fp, 0:32, odd * 128 : odd * 128 + 128] = a.astype(BF16)
                LHS[hi * FLO + fp, 32:64, odd * 128 : odd * 128 + 128] = b.astype(BF16)
        return c

    low64 = iota((128, 128), 1) < 64

    def correlate(slot):
        def some(g, c):
            for u in range(UNROLL):
                fp = g * UNROLL + u
                x = X[pl.ds(slot * 8, 8), fp].reshape(128, 128).astype(F32)
                rolled = pltpu.roll(x, 64, 1)
                zero = jnp.zeros_like(x)
                r0 = jnp.concatenate([jnp.where(low64, x, zero), jnp.where(low64, zero, rolled)], axis=0).astype(BF16)
                r1 = jnp.concatenate([jnp.where(low64, rolled, zero), jnp.where(low64, zero, x)], axis=0).astype(BF16)
                for hi, r in ((0, r0), (1, r1)):
                    f = hi * FLO + fp
                    O[pl.ds(f, 64, stride=PAD), :] = jnp.dot(LHS[f], r, preferred_element_type=F32)
            return c

        lax.fori_loop(0, FLO // UNROLL, some, 0)
        for k in range(2):
            for i in range(32):
                at = (k * 32 + i) * PAD
                out[k, slot, :, i * 128 : i * 128 + 128] = (O[at : at + 64, :] * 0.125).astype(BF16)

    pieces_in(first_forward, 0)
    forward(1, 0).start()
    pieces_in(first_back, 0)
    back(7, 0).start()
    lax.fori_loop(0, FLO, prepare, 0)
    correlate(0)
    pieces_in(first_forward, 4)
    forward(1, 1).start()
    pieces_in(first_back, 4)
    back(7, 1).start()
    correlate(8)
    correlate(1)
    correlate(7)
    forward(1, 0).wait_recv()
    forward(2, 0).start()
    back(7, 0).wait_recv()
    back(7, 1).wait_recv()
    back(6, 1).start()
    back(6, 0).start()
    forward(1, 1).wait_recv()
    forward(2, 1).start()
    correlate(2)
    correlate(6)
    forward(2, 0).wait_recv()
    forward(3, 0).start()
    back(6, 1).wait_recv()
    back(5, 1).start()
    forward(2, 1).wait_recv()
    correlate(3)
    back(6, 0).wait_recv()
    correlate(5)
    forward(3, 0).wait_recv()
    back(5, 1).wait_recv()
    correlate(4)

    halo.wait_send()

    def sent(n, c):
        @pl.when(n > 0)
        def _():
            a2a_copy(n // 2, n % 2).wait_send()

        first_forward(n).wait_send()
        exchange(n).wait_send()
        first_back(n).wait_send()
        return c

    lax.fori_loop(0, 8, sent, 0)
    for half in range(2):
        for slot in (1, 2):
            forward(slot, half).wait_send()
        for slot in (7, 6):
            back(slot, half).wait_send()
    forward(3, 0).wait_send()
    back(5, 1).wait_send()


def store(part, out, sem):
    copies = [
        pltpu.make_async_copy(part.at[k, s], out.at[k, s], sem.at[k, s]) for k in range(2) for s in range(STEPS)
    ]
    for copy in copies:
        copy.start()
    for copy in copies:
        copy.wait()


def body(spectra, quality):
    shape = jax.ShapeDtypeStruct((2, STEPS, 64, CB * CB), BF16)
    part = pl.pallas_call(
        kernel,
        out_shape=shape,
        in_specs=[pl.BlockSpec(memory_space=pltpu.HBM)] * 2,
        out_specs=pl.BlockSpec(memory_space=pltpu.VMEM),
        scratch_shapes=[
            pltpu.VMEM((2, WIN, CB, BAND), BF16),
            pltpu.VMEM((WIN, CB), jnp.int32),
            pltpu.VMEM((80, FLO, 16, 128), BF16),
            pltpu.VMEM((64, 64, 256), BF16),
            pltpu.VMEM((64 * PAD, 128), F32),
            pltpu.VMEM((4, WIN * CB, 128), F32),
            pltpu.VMEM((WIN * CB, BAND), BF16),
            pltpu.VMEM((WIN * CB, BAND), BF16),
            pltpu.VMEM((BAND, BAND), BF16),
            pltpu.VMEM((1024, 128), F32),
            pltpu.VMEM((128, 128), F32),
            pltpu.VMEM((128, 128), BF16),
            pltpu.VMEM((128, 128), BF16),
            pltpu.SemaphoreType.DMA((2,)),
            pltpu.SemaphoreType.DMA((2,)),
            pltpu.SemaphoreType.DMA((8,)),
            pltpu.SemaphoreType.DMA((9, 8)),
            pltpu.SemaphoreType.DMA((9, 8)),
        ],
        compiler_params=pltpu.CompilerParams(
            collective_id=0, has_side_effects=True, vmem_limit_bytes=32 * 1024 * 1024
        ),
        cost_estimate=pl.CostEstimate(flops=1300000000, bytes_accessed=11000000, transcendentals=262144),
    )(spectra, quality)
    result = pl.pallas_call(
        store,
        out_shape=shape,
        in_specs=[pl.BlockSpec(memory_space=pltpu.VMEM)],
        out_specs=pl.BlockSpec(memory_space=pl.ANY),
        scratch_shapes=[pltpu.SemaphoreType.DMA((2, STEPS))],
        compiler_params=pltpu.CompilerParams(vmem_limit_bytes=1024 * 1024),
    )(part)
    return result.reshape(1, 2, STEPS, 1, 64, CB * CB)


def solution(mesh):
    return jax.shard_map(
        body,
        mesh=mesh,
        in_specs=(P(None, "tm", "pair", "band"), P("tm", "pair")),
        out_specs=P("pair", None, None, "band", "tm", None),
        check_vma=False,
    )
```

```python
import jax
import jax.numpy as jnp
from jax import lax
from jax.experimental import pallas as pl
from jax.experimental.pallas import tpu as pltpu
from jax.sharding import PartitionSpec as P

MESH = pl.DeviceIdType.MESH
SMOOTH = 32
WIDTH = 2 * SMOOTH + 1
WIN = 8
CB = 64
BAND = 512
PIECES = 8
FLO = 32
STEPS = 9
LIMIT = 32
UNROLL = 8
SPLIT = 3
CUT = 24
PAD = 72
F32 = jnp.float32
BF16 = jnp.bfloat16


def iota(shape, dim):
    return lax.broadcasted_iota(jnp.int32, shape, dim)


def products(right, LHS, O, out):
    low64 = iota((128, 128), 1) < 64

    def some(g, c):
        for u in range(UNROLL):
            fp = g * UNROLL + u
            x = right(fp).reshape(128, 128).astype(F32)
            rolled = pltpu.roll(x, 64, 1)
            zero = jnp.zeros_like(x)
            r0 = jnp.concatenate([jnp.where(low64, x, zero), jnp.where(low64, zero, rolled)], axis=0).astype(BF16)
            r1 = jnp.concatenate([jnp.where(low64, rolled, zero), jnp.where(low64, zero, x)], axis=0).astype(BF16)
            for hi, r in ((0, r0), (1, r1)):
                f = hi * FLO + fp
                O[pl.ds(f, 64, stride=PAD), :] = jnp.dot(LHS[f], r, preferred_element_type=F32)
        return c

    lax.fori_loop(0, FLO // UNROLL, some, 0)
    for k in range(2):
        for i in range(32):
            at = (k * 32 + i) * PAD
            out(k)[:, i * 128 : i * 128 + 128] = (O[at : at + 64, :] * 0.125).astype(BF16)


def kernel(
    spec_in, quality_in, out, LHS, X4,
    spec, quality, X, O, SC, PH, PL, BM, W, T, halo_out, halo_in,
    in_sem, halo_sem, a2a_send, recv, send,
):
    p = lax.axis_index("pair")
    t = lax.axis_index("tm")
    band = lax.axis_index("band")
    y, core = t // 2, t % 2
    nxt, prv, opp = (p + 1) % 16, (p + 15) % 16, (p + 8) % 16
    z = p % 8
    wrap = z % 7 == 0
    far = p - z + 7 - z
    load_spec = pltpu.make_async_copy(spec_in, spec, in_sem.at[0])
    load_quality = pltpu.make_async_copy(quality_in, quality, in_sem.at[1])
    load_spec.start()
    load_quality.start()

    barrier = pltpu.get_barrier_semaphore()
    for target in (nxt, prv, opp):
        pl.semaphore_signal(barrier, inc=1, device_id={"pair": target}, device_id_type=MESH)
    for step in range(1, 8):
        pl.semaphore_signal(barrier, inc=1, device_id={"tm": (t + step) % 8}, device_id_type=MESH)
    pl.semaphore_signal(barrier, inc=1, device_id={"band": 1 - band}, device_id_type=MESH)

    @pl.when(wrap)
    def _():
        pl.semaphore_signal(barrier, inc=1, device_id={"pair": far}, device_id_type=MESH)

    BM[...] = jnp.where(jnp.abs(iota((BAND, BAND), 0) - iota((BAND, BAND), 1)) <= SMOOTH, 1.0, 0.0).astype(BF16)
    load_spec.wait()
    load_quality.wait()

    def power(w, lanes):
        re = spec[0, w, :, lanes].astype(F32)
        im = spec[1, w, :, lanes].astype(F32)
        return re * re + im * im

    group = iota((16, 128), 1) // 32
    for w in range(WIN):
        last = pltpu.roll(power(w, slice(BAND - 128, BAND)), 32, 1)
        first = power(w, slice(0, 128))
        edge = jnp.where(band == 0, last, first)
        packed = edge[0:16]
        for g in range(1, 4):
            packed = jnp.where(group == g, pltpu.roll(edge[16 * g : 16 * g + 16], 32 * g, 1), packed)
        halo_out[w * 16 : w * 16 + 16, :] = packed.astype(BF16)

    def split(w, c):
        pw = power(w, slice(None))
        hi = pw.astype(BF16)
        rows = pl.ds(pl.multiple_of(w * CB, CB), CB)
        PH[rows, :] = hi
        PL[rows, :] = (pw - hi.astype(F32)).astype(BF16)
        return c

    lax.fori_loop(0, WIN, split, 0)

    pl.semaphore_wait(barrier, jnp.where(wrap, 12, 11))
    halo = pltpu.make_async_remote_copy(
        src_ref=halo_out, dst_ref=halo_in, send_sem=halo_sem.at[0], recv_sem=halo_sem.at[1],
        device_id={"band": 1 - band}, device_id_type=MESH,
    )
    halo.start()

    def smooth(m, c):
        rows = pl.ds(pl.multiple_of(m * 128, 128), 128)
        total = jnp.dot(PH[rows, :], BM[...], preferred_element_type=F32)
        total += jnp.dot(PL[rows, :], BM[...], preferred_element_type=F32)
        for tile in range(4):
            SC[tile, rows, :] = total[:, tile * 128 : tile * 128 + 128]
        return c

    lax.fori_loop(0, WIN * CB // 128, smooth, 0)

    eye = iota((CB, CB), 0) == iota((CB, CB), 1)

    def column(w):
        return jnp.sum(jnp.where(eye, quality[w : w + 1, :].astype(F32), 0.0), axis=1, keepdims=True)

    def scale_of(total, w):
        return lax.rsqrt(total * (1.0 / WIDTH) + 1e-06) * column(w)

    def chip(o):
        dy = o ^ (o >> 1)
        return jnp.where(band == 1, y + dy, y - dy + 4) % 4

    def a2a_copy(o, dc):
        target = chip(o) * 2 + (core ^ dc)
        n = 2 * o + dc
        return pltpu.make_async_remote_copy(
            src_ref=X.at[72 + n], dst_ref=X.at[n], send_sem=a2a_send.at[n], recv_sem=recv.at[0, n],
            device_id={"tm": target}, device_id_type=MESH,
        )

    low = iota((CB, 128), 1) % 64 < 32

    def turn(tile, scales):
        lanes = pl.ds(pl.multiple_of(tile * 128, 128), 128)
        for w in range(WIN):
            scale = scales(w)
            re = spec[0, w, :, lanes].astype(F32) * scale
            im = spec[1, w, :, lanes].astype(F32) * scale
            top = jnp.where(low, re, pltpu.roll(im, 32, 1))
            bottom = jnp.where(low, pltpu.roll(re, 96, 1), im)
            turned = jnp.concatenate([top, bottom], axis=0).T
            for half in range(2):
                for k in range(2):
                    at = half * 64 + k * 32
                    W[pl.ds(half * 512 + k * 8 + w, FLO, stride=16), :] = turned[at : at + 32]

    def keep(o, dc, rows):
        X[jnp.where((o == 0) & (dc == 0), 0, 72 + 2 * o + dc)] = rows.astype(BF16).reshape(FLO, 16, 128)

    edge = jnp.where(band == 0, 7, 0)

    def whiten(o, c):
        tile = chip(o)
        turn(tile, lambda w: scale_of(SC[tile, w * CB : w * CB + CB, :], w))
        for half in range(2):
            keep(o, half ^ core, W[half * 512 : half * 512 + 512, :])
        for dc in range(2):
            @pl.when(((o > 0) | (dc > 0)) & (2 * tile + (core ^ dc) != edge))
            def _():
                a2a_copy(o, dc).start()

        return c

    def whiten_edge():
        src, dst = iota((128, 128), 0), iota((128, 128), 1)
        tile = edge // 2
        near = jnp.where(band == 0, dst - 96 - src % 32, src % 32 - dst) >= 0
        parts = []
        for g in range(4):
            ones = jnp.where((src // 32 == g) & near, 1.0, 0.0).astype(BF16)
            parts.append(jnp.dot(halo_in[...], ones, preferred_element_type=F32))

        def scales(w):
            more = jnp.concatenate([part[w * 16 : w * 16 + 16] for part in parts], axis=0)
            return scale_of(SC[tile, w * CB : w * CB + CB, :] + more, w)

        turn(tile, scales)
        dy, dc = jnp.where(band == 1, tile - y + 4, y - tile + 4) % 4, (edge % 2) ^ core
        o = dy ^ (dy >> 1)
        keep(o, dc, W[pl.ds(pl.multiple_of((edge % 2) * 512, 512), 512), :])

        @pl.when(t != edge)
        def _():
            a2a_copy(o, dc).start()

    def last_hop(src_slot, n, count, low, rows, target, row, sem):
        return pltpu.make_async_remote_copy(
            src_ref=X.at[pl.ds(src_slot * 8 + n, count), pl.ds(low, rows)],
            dst_ref=X4.at[pl.ds(n, count), pl.ds(low, rows)],
            send_sem=send.at[row, sem], recv_sem=recv.at[4, sem],
            device_id={"pair": target}, device_id_type=MESH,
        )

    def hop(src_slot, dst_slot, n, count, target, row, sem, recv_at):
        return pltpu.make_async_remote_copy(
            src_ref=X.at[pl.ds(src_slot * 8 + n, count)], dst_ref=X.at[pl.ds(dst_slot * 8 + n, count)],
            send_sem=send.at[row, sem], recv_sem=recv.at[dst_slot, recv_at],
            device_id={"pair": target}, device_id_type=MESH,
        )

    def first_forward(n):
        return hop(jnp.where(z == 7, 8, 0), 1, n, 1, jnp.where(z == 7, far, nxt), 0, n, n)

    def exchange(n):
        return hop(0, 8, n, 1, opp, 1, n, n)

    def first_back(n):
        return hop(jnp.where(z == 0, 0, 8), 7, n, 1, jnp.where(z == 0, far, prv), 2, n, n)

    def own_step(n):
        exchange(n).start()

        @pl.when(z != 7)
        def _():
            first_forward(n).start()

        @pl.when(z == 0)
        def _():
            first_back(n).start()

    def opposite_step(n):
        exchange(n).wait_recv()

        @pl.when(z == 7)
        def _():
            first_forward(n).start()

        @pl.when(z != 0)
        def _():
            first_back(n).start()

    def pieces_in(copy, start):
        def one(n, c):
            copy(n).wait_recv()
            return c

        lax.fori_loop(start, start + 4, one, 0)

    def forward(slot, half):
        return hop(slot, slot + 1, 4 * half, 4, nxt, 2 + slot, half, half)

    def back(slot, half):
        return hop(slot, slot - 1, 4 * half, 4, prv, 13 - slot, half, half)

    def last_forward(part):
        if part == 0:
            return last_hop(3, 0, SPLIT, 0, FLO, nxt, 5, 0)
        return last_hop(3, SPLIT, 1, 0, CUT, nxt, 5, 1)

    def last_back(part):
        if part == 0:
            return last_hop(5, SPLIT + 1, PIECES - 1 - SPLIT, 0, FLO, prv, 8, 2)
        return last_hop(5, SPLIT, 1, CUT, FLO - CUT, prv, 8, 3)

    lane = iota((CB // 2, 128), 1)

    def prepare(fp, c):
        x = X[0:8, fp].reshape(128, 128).astype(F32)
        T[...] = x.T
        for hi in range(2):
            for odd in range(2):
                a = T[pl.ds(hi * 64 + odd, 32, stride=2), :]
                b = jnp.where(lane % 16 < 8, pltpu.roll(a, 120, 1), -pltpu.roll(a, 8, 1))
                LHS[hi * FLO + fp, 0:32, odd * 128 : odd * 128 + 128] = a.astype(BF16)
                LHS[hi * FLO + fp, 32:64, odd * 128 : odd * 128 + 128] = b.astype(BF16)
        return c

    def correlate(slot):
        place = slot - (slot > 4)
        products(
            lambda fp: X[pl.ds(slot * 8, 8), fp], LHS, O,
            lambda k: out.at[k, place],
        )

    whiten(0, 0)

    @pl.when(t != edge)
    def _():
        own_step(0)

    lax.fori_loop(1, 4, whiten, 0)

    @pl.when(t != edge)
    def _():
        a2a_copy(0, 1).wait_recv()
        own_step(1)

    halo.wait_recv()
    whiten_edge()

    @pl.when(t == edge)
    def _():
        own_step(0)
        a2a_copy(0, 1).wait_recv()
        own_step(1)

    def early(n, c):
        a2a_copy(n // 2, n % 2).wait_recv()
        own_step(n)
        opposite_step(n - 2)
        return c

    lax.fori_loop(2, 8, early, 0)
    pieces_in(first_forward, 0)
    forward(1, 0).start()
    opposite_step(6)
    opposite_step(7)
    pieces_in(first_back, 0)
    back(7, 0).start()
    lax.fori_loop(0, FLO, prepare, 0)
    correlate(0)
    pieces_in(first_forward, 4)
    forward(1, 1).start()
    pieces_in(first_back, 4)
    back(7, 1).start()
    correlate(8)
    correlate(1)
    correlate(7)
    forward(1, 0).wait_recv()
    forward(2, 0).start()
    back(7, 0).wait_recv()
    back(7, 1).wait_recv()
    back(6, 1).start()
    back(6, 0).start()
    forward(1, 1).wait_recv()
    forward(2, 1).start()
    correlate(2)
    correlate(6)
    forward(2, 0).wait_recv()
    last_forward(0).start()
    back(6, 1).wait_recv()
    last_back(0).start()
    forward(2, 1).wait_recv()
    last_forward(1).start()
    back(6, 0).wait_recv()
    last_back(1).start()
    correlate(3)
    correlate(5)
    for part in range(2):
        last_forward(part).wait_recv()
        last_back(part).wait_recv()
    halo.wait_send()

    def sent(n, c):
        @pl.when(n > 0)
        def _():
            a2a_copy(n // 2, n % 2).wait_send()

        first_forward(n).wait_send()
        exchange(n).wait_send()
        first_back(n).wait_send()
        return c

    lax.fori_loop(0, 8, sent, 0)
    for half in range(2):
        for slot in (1, 2):
            forward(slot, half).wait_send()
        for slot in (7, 6):
            back(slot, half).wait_send()
    for part in range(2):
        last_forward(part).wait_send()
        last_back(part).wait_send()


def finish(part, LHS, X4, out, O, last, sem):
    copies = [
        pltpu.make_async_copy(part.at[k, s], out.at[k, s + (s > 3)], sem.at[k, s])
        for s in range(STEPS - 1) for k in range(2)
    ]
    for copy in copies:
        copy.start()
    products(lambda fp: X4[:, fp], LHS, O, lambda k: last.at[k])
    for k in range(2):
        copies.append(pltpu.make_async_copy(last.at[k], out.at[k, 4], sem.at[k, STEPS - 1]))
        copies[-1].start()
    for copy in copies:
        copy.wait()


def body(spectra, quality):
    in_vmem = pl.BlockSpec(memory_space=pltpu.VMEM)
    part, left, last = pl.pallas_call(
        kernel,
        out_shape=(
            jax.ShapeDtypeStruct((2, STEPS - 1, 64, CB * CB), BF16),
            jax.ShapeDtypeStruct((64, 64, 256), BF16),
            jax.ShapeDtypeStruct((PIECES, FLO, 16, 128), BF16),
        ),
        in_specs=[pl.BlockSpec(memory_space=pltpu.HBM)] * 2,
        out_specs=(in_vmem,) * 3,
        scratch_shapes=[
            pltpu.VMEM((2, WIN, CB, BAND), BF16),
            pltpu.VMEM((WIN, CB), jnp.int32),
            pltpu.VMEM((80, FLO, 16, 128), BF16),
            pltpu.VMEM((64 * PAD, 128), F32),
            pltpu.VMEM((4, WIN * CB, 128), F32),
            pltpu.VMEM((WIN * CB, BAND), BF16),
            pltpu.VMEM((WIN * CB, BAND), BF16),
            pltpu.VMEM((BAND, BAND), BF16),
            pltpu.VMEM((1024, 128), F32),
            pltpu.VMEM((128, 128), F32),
            pltpu.VMEM((128, 128), BF16),
            pltpu.VMEM((128, 128), BF16),
            pltpu.SemaphoreType.DMA((2,)),
            pltpu.SemaphoreType.DMA((2,)),
            pltpu.SemaphoreType.DMA((8,)),
            pltpu.SemaphoreType.DMA((9, 8)),
            pltpu.SemaphoreType.DMA((9, 8)),
        ],
        compiler_params=pltpu.CompilerParams(
            collective_id=0, has_side_effects=True, vmem_limit_bytes=LIMIT * 1024 * 1024
        ),
        cost_estimate=pl.CostEstimate(flops=1300000000, bytes_accessed=11000000, transcendentals=262144),
    )(spectra, quality)
    result = pl.pallas_call(
        finish,
        out_shape=jax.ShapeDtypeStruct((2, STEPS, 64, CB * CB), BF16),
        in_specs=[in_vmem] * 3,
        out_specs=pl.BlockSpec(memory_space=pl.ANY),
        scratch_shapes=[
            pltpu.VMEM((64 * PAD, 128), F32),
            pltpu.VMEM((2, 64, CB * CB), BF16),
            pltpu.SemaphoreType.DMA((2, STEPS)),
        ],
        compiler_params=pltpu.CompilerParams(vmem_limit_bytes=8 * 1024 * 1024),
    )(part, left, last)
    return result.reshape(1, 2, STEPS, 1, 64, CB * CB)


def solution(mesh):
    return jax.shard_map(
        body,
        mesh=mesh,
        in_specs=(P(None, "tm", "pair", "band"), P("tm", "pair")),
        out_specs=P("pair", None, None, "band", "tm", None),
        check_vma=False,
    )
```

```python
import jax
import jax.numpy as jnp
from jax import lax
from jax.experimental import pallas as pl
from jax.experimental.pallas import tpu as pltpu
from jax.sharding import PartitionSpec as P

MESH = pl.DeviceIdType.MESH
SMOOTH = 32
WIDTH = 2 * SMOOTH + 1
WIN = 8
CB = 64
BAND = 512
PIECES = 8
HALF = 16
FLO = 32
STEPS = 9
LAG = 1
LIMIT = 32
UNROLL = 8
SPLIT = 3
CUT = 24
PAD = 72
F32 = jnp.float32
BF16 = jnp.bfloat16


def iota(shape, dim):
    return lax.broadcasted_iota(jnp.int32, shape, dim)


def products(right, LHS, O, out):
    low64 = iota((128, 128), 1) < 64

    def some(g, c):
        for u in range(UNROLL):
            fp = g * UNROLL + u
            x = right(fp).reshape(128, 128).astype(F32)
            rolled = pltpu.roll(x, 64, 1)
            zero = jnp.zeros_like(x)
            r0 = jnp.concatenate([jnp.where(low64, x, zero), jnp.where(low64, zero, rolled)], axis=0).astype(BF16)
            r1 = jnp.concatenate([jnp.where(low64, rolled, zero), jnp.where(low64, zero, x)], axis=0).astype(BF16)
            for hi, r in ((0, r0), (1, r1)):
                f = fp + (fp // HALF + hi) * HALF
                O[pl.ds(f, 64, stride=PAD), :] = jnp.dot(LHS[hi * FLO + fp], r, preferred_element_type=F32)
        return c

    lax.fori_loop(0, FLO // UNROLL, some, 0)
    for k in range(2):
        for i in range(32):
            at = (k * 32 + i) * PAD
            out(k)[:, i * 128 : i * 128 + 128] = (O[at : at + 64, :] * 0.125).astype(BF16)


def kernel(
    spec_in, quality_in, out, LHS, X4,
    spec, quality, X, O, SC, PH, PL, BM, W, T, halo_out, halo_in,
    in_sem, halo_sem, a2a_send, recv, send,
):
    p = lax.axis_index("pair")
    t = lax.axis_index("tm")
    band = lax.axis_index("band")
    y, core = t // 2, t % 2
    nxt, prv, opp = (p + 1) % 16, (p + 15) % 16, (p + 8) % 16
    z = p % 8
    wrap = z % 7 == 0
    far = p - z + 7 - z
    load_spec = pltpu.make_async_copy(spec_in, spec, in_sem.at[0])
    load_quality = pltpu.make_async_copy(quality_in, quality, in_sem.at[1])
    load_spec.start()
    load_quality.start()

    barrier = pltpu.get_barrier_semaphore()
    for target in (nxt, prv, opp):
        pl.semaphore_signal(barrier, inc=1, device_id={"pair": target}, device_id_type=MESH)
    for step in range(1, 8):
        pl.semaphore_signal(barrier, inc=1, device_id={"tm": (t + step) % 8}, device_id_type=MESH)
    pl.semaphore_signal(barrier, inc=1, device_id={"band": 1 - band}, device_id_type=MESH)

    @pl.when(wrap)
    def _():
        pl.semaphore_signal(barrier, inc=1, device_id={"pair": far}, device_id_type=MESH)

    BM[...] = jnp.where(jnp.abs(iota((BAND, BAND), 0) - iota((BAND, BAND), 1)) <= SMOOTH, 1.0, 0.0).astype(BF16)
    load_spec.wait()
    load_quality.wait()

    def power(w, lanes):
        re = spec[0, w, :, lanes].astype(F32)
        im = spec[1, w, :, lanes].astype(F32)
        return re * re + im * im

    group = iota((16, 128), 1) // 32
    for w in range(WIN):
        last = pltpu.roll(power(w, slice(BAND - 128, BAND)), 32, 1)
        first = power(w, slice(0, 128))
        edge = jnp.where(band == 0, last, first)
        packed = edge[0:16]
        for g in range(1, 4):
            packed = jnp.where(group == g, pltpu.roll(edge[16 * g : 16 * g + 16], 32 * g, 1), packed)
        halo_out[w * 16 : w * 16 + 16, :] = packed.astype(BF16)

    def split(w, c):
        pw = power(w, slice(None))
        hi = pw.astype(BF16)
        rows = pl.ds(pl.multiple_of(w * CB, CB), CB)
        PH[rows, :] = hi
        PL[rows, :] = (pw - hi.astype(F32)).astype(BF16)
        return c

    lax.fori_loop(0, WIN, split, 0)

    def smooth(m, c):
        rows = pl.ds(pl.multiple_of(m * 128, 128), 128)
        total = jnp.dot(PH[rows, :], BM[...], preferred_element_type=F32)
        total += jnp.dot(PL[rows, :], BM[...], preferred_element_type=F32)
        for tile in range(4):
            SC[tile, rows, :] = total[:, tile * 128 : tile * 128 + 128]
        return c

    lax.fori_loop(0, WIN * CB // 128, smooth, 0)

    eye = iota((CB, CB), 0) == iota((CB, CB), 1)

    def column(w):
        return jnp.sum(jnp.where(eye, quality[w : w + 1, :].astype(F32), 0.0), axis=1, keepdims=True)

    def scale_of(total, w):
        return lax.rsqrt(total * (1.0 / WIDTH) + 1e-06) * column(w)

    def chip(o):
        dy = o ^ (o >> 1)
        return jnp.where(band == 1, y + dy, y - dy + 4) % 4

    def place(o, dc):
        return jnp.where(o == 0, dc, jnp.where(o == 3, 6 + dc, 1 + o + 2 * dc))

    def a2a_target(n):
        o = jnp.where(n < 2, 0, jnp.where(n < 6, 1 + n % 2, 3))
        dc = jnp.where(n < 2, n, jnp.where(n < 4, 0, jnp.where(n < 6, 1, n - 6)))
        return 2 * chip(o) + (core ^ dc)

    def a2a_copy(n, h):
        rows = pl.ds(HALF * h, HALF)
        return pltpu.make_async_remote_copy(
            src_ref=X.at[72 + n, rows], dst_ref=X.at[n, rows], send_sem=a2a_send.at[2 * n + h], recv_sem=recv.at[0, 2 * n + h],
            device_id={"tm": a2a_target(n)}, device_id_type=MESH,
        )

    low = iota((CB, 128), 1) % 32 < 16

    def turn(tile, scales):
        lanes = pl.ds(pl.multiple_of(tile * 128, 128), 128)
        for w in range(WIN):
            scale = scales(w)
            re = spec[0, w, :, lanes].astype(F32) * scale
            im = spec[1, w, :, lanes].astype(F32) * scale
            top = jnp.where(low, re, pltpu.roll(im, 16, 1))
            bottom = jnp.where(low, pltpu.roll(re, 112, 1), im)
            turned = jnp.concatenate([top, bottom], axis=0).T
            for half in range(2):
                for h in range(2):
                    for k in range(2):
                        at = half * 64 + h * 32 + k * 16
                        W[pl.ds(half * 512 + h * 256 + k * 8 + w, HALF, stride=16), :] = turned[at : at + 16]

    def keep(o, dc, rows):
        n = place(o, dc)
        X[jnp.where(n == 0, 0, 72 + n)] = rows.astype(BF16).reshape(FLO, 16, 128)

    edge = jnp.where(band == 0, 7, 0)
    late = 1 - band

    def whiten(o, c):
        tile = chip(o)
        turn(tile, lambda w: scale_of(SC[tile, w * CB : w * CB + CB, :], w))
        for half in range(2):
            keep(o, half ^ core, W[half * 512 : half * 512 + 512, :])
        return c

    def give(n):
        for h in range(2):
            @pl.when((a2a_target(n) != edge) | (late != h))
            def _():
                a2a_copy(n, h).start()

    def whiten_edge():
        src, dst = iota((128, 128), 0), iota((128, 128), 1)
        tile = edge // 2
        near = jnp.where(band == 0, dst - 96 - src % 32, src % 32 - dst) >= 0
        parts = []
        for g in range(4):
            ones = jnp.where((src // 32 == g) & near, 1.0, 0.0).astype(BF16)
            parts.append(jnp.dot(halo_in[...], ones, preferred_element_type=F32))

        def scales(w):
            more = jnp.concatenate([part[w * 16 : w * 16 + 16] for part in parts], axis=0)
            return scale_of(SC[tile, w * CB : w * CB + CB, :] + more, w)

        turn(tile, scales)
        dy, dc = jnp.where(band == 1, tile - y + 4, y - tile + 4) % 4, (edge % 2) ^ core
        o = dy ^ (dy >> 1)
        n = place(o, dc)
        rows = W[pl.ds(pl.multiple_of((edge % 2) * 512 + late * 256, 256), 256), :]
        X[jnp.where(n == 0, 0, 72 + n), pl.ds(HALF * late, HALF)] = rows.astype(BF16).reshape(HALF, 16, 128)

        @pl.when(t != edge)
        def _():
            a2a_copy(n, late).start()

    def last_hop(src_slot, n, count, low, rows, target, row, sem):
        return pltpu.make_async_remote_copy(
            src_ref=X.at[pl.ds(src_slot * 8 + n, count), pl.ds(low, rows)],
            dst_ref=X4.at[pl.ds(n, count), pl.ds(low, rows)],
            send_sem=send.at[row, sem], recv_sem=recv.at[4, sem],
            device_id={"pair": target}, device_id_type=MESH,
        )

    def hop(src_slot, dst_slot, n, count, target, row, sem, recv_at):
        return pltpu.make_async_remote_copy(
            src_ref=X.at[pl.ds(src_slot * 8 + n, count)], dst_ref=X.at[pl.ds(dst_slot * 8 + n, count)],
            send_sem=send.at[row, sem], recv_sem=recv.at[dst_slot, recv_at],
            device_id={"pair": target}, device_id_type=MESH,
        )

    def half_hop(src_slot, dst_slot, n, h, target, row):
        rows = pl.ds(HALF * h, HALF)
        return pltpu.make_async_remote_copy(
            src_ref=X.at[src_slot * 8 + n, rows], dst_ref=X.at[dst_slot * 8 + n, rows],
            send_sem=send.at[row, 2 * n + h], recv_sem=recv.at[dst_slot, 2 * n + h],
            device_id={"pair": target}, device_id_type=MESH,
        )

    def first_forward(n, h):
        return half_hop(jnp.where(z == 7, 8, 0), 1, n, h, jnp.where(z == 7, far, nxt), 0)

    def exchange(n, h):
        return half_hop(0, 8, n, h, opp, 1)

    def first_back(n, h):
        return half_hop(jnp.where(z == 0, 0, 8), 7, n, h, jnp.where(z == 0, far, prv), 2)

    lag = jnp.where(t == edge, LAG, 0)
    early_half = jnp.where(t == edge, 1 - late, 0)

    def halves(n, do):
        @pl.when(n < 8)
        def _():
            do(n, early_half)

        @pl.when((n >= lag) & (n - lag < 8))
        def _():
            do(n - lag, 1 - early_half)

    def own_half(n, h):
        @pl.when(n > 0)
        def _():
            a2a_copy(n, h).wait_recv()

        exchange(n, h).start()

        @pl.when(z != 7)
        def _():
            first_forward(n, h).start()

        @pl.when(z == 0)
        def _():
            first_back(n, h).start()

    def opposite_half(n, h):
        exchange(n, h).wait_recv()

        @pl.when(z == 7)
        def _():
            first_forward(n, h).start()

        @pl.when(z != 0)
        def _():
            first_back(n, h).start()

    def pieces_in(copy, start, count=4):
        def one(n, c):
            for h in range(2):
                copy(n, h).wait_recv()
            return c

        lax.fori_loop(start, start + count, one, 0)

    def forward(slot, half):
        return hop(slot, slot + 1, 4 * half, 4, nxt, 2 + slot, half, half)

    def back(slot, quarter):
        return hop(slot, slot - 1, 2 * quarter, 2, prv, 13 - slot, quarter, quarter)

    def last_forward(part):
        if part == 0:
            return last_hop(3, 0, SPLIT, 0, FLO, nxt, 5, 0)
        return last_hop(3, SPLIT, 1, 0, CUT, nxt, 5, 1)

    def last_back(part):
        if part < 2:
            return last_hop(5, 4 + 2 * part, 2, 0, FLO, prv, 8, 2 + part)
        return last_hop(5, SPLIT, 1, CUT, FLO - CUT, prv, 8, 4)

    lane = iota((CB // 2, 128), 1)

    def prepare(fp, c):
        x = X[0:8, fp].reshape(128, 128).astype(F32)
        T[...] = x.T
        for hi in range(2):
            for odd in range(2):
                a = T[pl.ds(hi * 64 + odd, 32, stride=2), :]
                b = jnp.where(lane % 16 < 8, pltpu.roll(a, 120, 1), -pltpu.roll(a, 8, 1))
                LHS[hi * FLO + fp, 0:32, odd * 128 : odd * 128 + 128] = a.astype(BF16)
                LHS[hi * FLO + fp, 32:64, odd * 128 : odd * 128 + 128] = b.astype(BF16)
        return c

    def correlate(slot):
        place = slot - (slot > 4)
        products(
            lambda fp: X[pl.ds(slot * 8, 8), fp], LHS, O,
            lambda k: out.at[k, place],
        )

    whiten(0, 0)
    pl.semaphore_wait(barrier, jnp.where(wrap, 12, 11))
    halo = pltpu.make_async_remote_copy(
        src_ref=halo_out, dst_ref=halo_in, send_sem=halo_sem.at[0], recv_sem=halo_sem.at[1],
        device_id={"band": 1 - band}, device_id_type=MESH,
    )
    halo.start()
    give(1)
    halves(0, own_half)
    whiten(1, 0)
    give(2)
    whiten(2, 0)
    give(3)
    whiten(3, 0)

    @pl.when(t != edge)
    def _():
        halves(1, own_half)

    @pl.when(t == edge)
    def _():
        own_half(1, early_half)

    halo.wait_recv()
    whiten_edge()

    @pl.when(t == edge)
    def _():
        own_half(0, late)

    give(4)
    give(5)

    @pl.when(t == edge)
    def _():
        give(6)
        give(7)

    halves(0, opposite_half)

    def early(n, c):
        halves(n, own_half)

        @pl.when((n == 3) & (t != edge))
        def _():
            give(6)
            give(7)

        @pl.when(n == 8)
        def _():
            pieces_in(first_forward, 0)
            forward(1, 0).start()

        @pl.when(n > 2)
        def _():
            halves(n - 2, opposite_half)

        return c

    lax.fori_loop(2, 10 + LAG, early, 0)
    for quarter in (1, 2):
        pieces_in(first_back, 2 * quarter, 2)
        back(7, quarter).start()
    lax.fori_loop(0, FLO, prepare, 0)
    correlate(0)
    pieces_in(first_forward, 4)
    forward(1, 1).start()
    for quarter in (3, 0):
        pieces_in(first_back, 2 * quarter, 2)
        back(7, quarter).start()
    correlate(8)
    correlate(1)
    correlate(7)
    forward(1, 0).wait_recv()
    forward(2, 0).start()
    for quarter in (2, 3):
        back(7, quarter).wait_recv()
        back(6, quarter).start()
    forward(1, 1).wait_recv()
    forward(2, 1).start()
    correlate(2)
    for quarter in (0, 1):
        back(7, quarter).wait_recv()
        back(6, quarter).start()
    correlate(6)
    forward(2, 0).wait_recv()
    last_forward(0).start()
    last_forward(1).start()
    for part in range(2):
        back(6, 2 + part).wait_recv()
        last_back(part).start()
    forward(2, 1).wait_recv()
    correlate(3)
    for quarter in (0, 1):
        back(6, quarter).wait_recv()
    last_back(2).start()
    correlate(5)
    for part in range(2):
        last_forward(part).wait_recv()
    for part in range(3):
        last_back(part).wait_recv()
    halo.wait_send()

    def sent(n, c):
        for h in range(2):
            @pl.when(n > 0)
            def _():
                a2a_copy(n, h).wait_send()

            first_forward(n, h).wait_send()
            exchange(n, h).wait_send()
            first_back(n, h).wait_send()
        return c

    lax.fori_loop(0, 8, sent, 0)
    for half in range(2):
        for slot in (1, 2):
            forward(slot, half).wait_send()
    for quarter in range(4):
        for slot in (7, 6):
            back(slot, quarter).wait_send()
    for part in range(2):
        last_forward(part).wait_send()
    for part in range(3):
        last_back(part).wait_send()


def finish(part, LHS, X4, out, O, last, sem):
    copies = [
        pltpu.make_async_copy(part.at[k, s], out.at[k, s + (s > 3)], sem.at[k, s])
        for s in range(STEPS - 1) for k in range(2)
    ]
    for copy in copies:
        copy.start()
    products(lambda fp: X4[:, fp], LHS, O, lambda k: last.at[k])
    for k in range(2):
        copies.append(pltpu.make_async_copy(last.at[k], out.at[k, 4], sem.at[k, STEPS - 1]))
        copies[-1].start()
    for copy in copies:
        copy.wait()


def body(spectra, quality):
    in_vmem = pl.BlockSpec(memory_space=pltpu.VMEM)
    part, left, last = pl.pallas_call(
        kernel,
        out_shape=(
            jax.ShapeDtypeStruct((2, STEPS - 1, 64, CB * CB), BF16),
            jax.ShapeDtypeStruct((64, 64, 256), BF16),
            jax.ShapeDtypeStruct((PIECES, FLO, 16, 128), BF16),
        ),
        in_specs=[pl.BlockSpec(memory_space=pltpu.HBM)] * 2,
        out_specs=(in_vmem,) * 3,
        scratch_shapes=[
            pltpu.VMEM((2, WIN, CB, BAND), BF16),
            pltpu.VMEM((WIN, CB), jnp.int32),
            pltpu.VMEM((80, FLO, 16, 128), BF16),
            pltpu.VMEM((64 * PAD, 128), F32),
            pltpu.VMEM((4, WIN * CB, 128), F32),
            pltpu.VMEM((WIN * CB, BAND), BF16),
            pltpu.VMEM((WIN * CB, BAND), BF16),
            pltpu.VMEM((BAND, BAND), BF16),
            pltpu.VMEM((1024, 128), F32),
            pltpu.VMEM((128, 128), F32),
            pltpu.VMEM((128, 128), BF16),
            pltpu.VMEM((128, 128), BF16),
            pltpu.SemaphoreType.DMA((2,)),
            pltpu.SemaphoreType.DMA((2,)),
            pltpu.SemaphoreType.DMA((16,)),
            pltpu.SemaphoreType.DMA((9, 16)),
            pltpu.SemaphoreType.DMA((9, 16)),
        ],
        compiler_params=pltpu.CompilerParams(
            collective_id=0, has_side_effects=True, vmem_limit_bytes=LIMIT * 1024 * 1024
        ),
        cost_estimate=pl.CostEstimate(flops=1300000000, bytes_accessed=11000000, transcendentals=262144),
    )(*(pltpu.with_memory_space_constraint(x, pltpu.HBM) for x in (spectra, quality)))
    result = pl.pallas_call(
        finish,
        out_shape=jax.ShapeDtypeStruct((2, STEPS, 64, CB * CB), BF16),
        in_specs=[in_vmem] * 3,
        out_specs=pl.BlockSpec(memory_space=pl.ANY),
        scratch_shapes=[
            pltpu.VMEM((64 * PAD, 128), F32),
            pltpu.VMEM((2, 64, CB * CB), BF16),
            pltpu.SemaphoreType.DMA((2, STEPS)),
        ],
        compiler_params=pltpu.CompilerParams(vmem_limit_bytes=8 * 1024 * 1024),
    )(part, left, last)
    return result.reshape(1, 2, STEPS, 1, 64, CB * CB)


def solution(mesh):
    return jax.shard_map(
        body,
        mesh=mesh,
        in_specs=(P(None, "tm", "pair", "band"), P("tm", "pair")),
        out_specs=P("pair", None, None, "band", "tm", None),
        check_vma=False,
    )
```

```python
import jax
import jax.numpy as jnp
from jax import lax
from jax.experimental import pallas as pl
from jax.experimental.pallas import tpu as pltpu
from jax.sharding import PartitionSpec as P

MESH = pl.DeviceIdType.MESH
SMOOTH = 32
WIDTH = 2 * SMOOTH + 1
WIN = 8
CB = 64
BAND = 512
PIECES = 8
HALF = 16
FLO = 32
STEPS = 9
LAG = 1
LIMIT = 32
UNROLL = 8
SPLIT = 3
CUT = 24
PAD = 72
F32 = jnp.float32
BF16 = jnp.bfloat16


def iota(shape, dim):
    return lax.broadcasted_iota(jnp.int32, shape, dim)


def products(right, LHS, O, out):
    low64 = iota((128, 128), 1) < 64

    def some(g, c):
        for u in range(UNROLL):
            fp = g * UNROLL + u
            x = right(fp).reshape(128, 128).astype(F32)
            rolled = pltpu.roll(x, 64, 1)
            zero = jnp.zeros_like(x)
            r0 = jnp.concatenate([jnp.where(low64, x, zero), jnp.where(low64, zero, rolled)], axis=0).astype(BF16)
            r1 = jnp.concatenate([jnp.where(low64, rolled, zero), jnp.where(low64, zero, x)], axis=0).astype(BF16)
            for hi, r in ((0, r0), (1, r1)):
                f = fp + (fp // HALF + hi) * HALF
                O[pl.ds(f, 64, stride=PAD), :] = jnp.dot(LHS[hi * FLO + fp], r, preferred_element_type=F32)
        return c

    lax.fori_loop(0, FLO // UNROLL, some, 0)
    for k in range(2):
        for i in range(32):
            at = (k * 32 + i) * PAD
            out(k)[:, i * 128 : i * 128 + 128] = (O[at : at + 64, :] * 0.125).astype(BF16)


def kernel(
    spec_in, quality_in, out, LHS, X4,
    spec, quality, X, O, SC, PH, PL, BM, W, T, halo_out, halo_in,
    in_sem, halo_sem, a2a_send, recv, send,
):
    p = lax.axis_index("pair")
    t = lax.axis_index("tm")
    band = lax.axis_index("band")
    y, core = t // 2, t % 2
    nxt, prv, opp = (p + 1) % 16, (p + 15) % 16, (p + 8) % 16
    z = p % 8
    wrap = z % 7 == 0
    far = p - z + 7 - z
    load_spec = pltpu.make_async_copy(spec_in, spec, in_sem.at[0])
    load_quality = pltpu.make_async_copy(quality_in, quality, in_sem.at[1])
    load_spec.start()
    load_quality.start()

    barrier = pltpu.get_barrier_semaphore()
    for target in (nxt, prv, opp):
        pl.semaphore_signal(barrier, inc=1, device_id={"pair": target}, device_id_type=MESH)
    for step in range(1, 8):
        pl.semaphore_signal(barrier, inc=1, device_id={"tm": (t + step) % 8}, device_id_type=MESH)
    pl.semaphore_signal(barrier, inc=1, device_id={"band": 1 - band}, device_id_type=MESH)

    @pl.when(wrap)
    def _():
        pl.semaphore_signal(barrier, inc=1, device_id={"pair": far}, device_id_type=MESH)

    BM[...] = jnp.where(jnp.abs(iota((BAND, BAND), 0) - iota((BAND, BAND), 1)) <= SMOOTH, 1.0, 0.0).astype(BF16)
    load_spec.wait()
    load_quality.wait()

    def power(w, lanes):
        re = spec[0, w, :, lanes].astype(F32)
        im = spec[1, w, :, lanes].astype(F32)
        return re * re + im * im

    group = iota((16, 128), 1) // 32
    for w in range(WIN):
        last = pltpu.roll(power(w, slice(BAND - 128, BAND)), 32, 1)
        first = power(w, slice(0, 128))
        edge = jnp.where(band == 0, last, first)
        packed = edge[0:16]
        for g in range(1, 4):
            packed = jnp.where(group == g, pltpu.roll(edge[16 * g : 16 * g + 16], 32 * g, 1), packed)
        halo_out[w * 16 : w * 16 + 16, :] = packed.astype(BF16)

    def split(w, c):
        pw = power(w, slice(None))
        hi = pw.astype(BF16)
        rows = pl.ds(pl.multiple_of(w * CB, CB), CB)
        PH[rows, :] = hi
        PL[rows, :] = (pw - hi.astype(F32)).astype(BF16)
        return c

    lax.fori_loop(0, WIN, split, 0)

    def smooth(m, c):
        rows = pl.ds(pl.multiple_of(m * 128, 128), 128)
        total = jnp.dot(PH[rows, :], BM[...], preferred_element_type=F32)
        total += jnp.dot(PL[rows, :], BM[...], preferred_element_type=F32)
        for tile in range(4):
            SC[tile, rows, :] = total[:, tile * 128 : tile * 128 + 128]
        return c

    lax.fori_loop(0, WIN * CB // 128, smooth, 0)

    eye = iota((CB, CB), 0) == iota((CB, CB), 1)

    def column(w):
        return jnp.sum(jnp.where(eye, quality[w : w + 1, :].astype(F32), 0.0), axis=1, keepdims=True)

    def scale_of(total, w):
        return lax.rsqrt(total * (1.0 / WIDTH) + 1e-06) * column(w)

    def chip(o):
        dy = o ^ (o >> 1)
        return jnp.where(band == 1, y + dy, y - dy + 4) % 4

    def place(o, dc):
        return jnp.where(o == 0, dc, jnp.where(o == 3, 6 + dc, 1 + o + 2 * dc))

    def a2a_target(n):
        o = jnp.where(n < 2, 0, jnp.where(n < 6, 1 + n % 2, 3))
        dc = jnp.where(n < 2, n, jnp.where(n < 4, 0, jnp.where(n < 6, 1, n - 6)))
        return 2 * chip(o) + (core ^ dc)

    def a2a_copy(n, h):
        rows = pl.ds(HALF * h, HALF)
        return pltpu.make_async_remote_copy(
            src_ref=X.at[72 + n, rows], dst_ref=X.at[n, rows], send_sem=a2a_send.at[2 * n + h], recv_sem=recv.at[0, 2 * n + h],
            device_id={"tm": a2a_target(n)}, device_id_type=MESH,
        )

    low = iota((CB, 128), 1) % 32 < 16

    def turn(tile, scales):
        lanes = pl.ds(pl.multiple_of(tile * 128, 128), 128)
        for w in range(WIN):
            scale = scales(w)
            re = spec[0, w, :, lanes].astype(F32) * scale
            im = spec[1, w, :, lanes].astype(F32) * scale
            top = jnp.where(low, re, pltpu.roll(im, 16, 1))
            bottom = jnp.where(low, pltpu.roll(re, 112, 1), im)
            turned = jnp.concatenate([top, bottom], axis=0).T
            for half in range(2):
                for h in range(2):
                    for k in range(2):
                        at = half * 64 + h * 32 + k * 16
                        W[pl.ds(half * 512 + h * 256 + k * 8 + w, HALF, stride=16), :] = turned[at : at + 16]

    def keep(o, dc, rows):
        n = place(o, dc)
        X[jnp.where(n == 0, 0, 72 + n)] = rows.astype(BF16).reshape(FLO, 16, 128)

    edge = jnp.where(band == 0, 7, 0)
    late = 1 - band

    def whiten(o, c):
        tile = chip(o)
        turn(tile, lambda w: scale_of(SC[tile, w * CB : w * CB + CB, :], w))
        for half in range(2):
            keep(o, half ^ core, W[half * 512 : half * 512 + 512, :])
        return c

    def give(n):
        for h in range(2):
            @pl.when((a2a_target(n) != edge) | (late != h))
            def _():
                a2a_copy(n, h).start()

    def whiten_edge():
        src, dst = iota((128, 128), 0), iota((128, 128), 1)
        tile = edge // 2
        near = jnp.where(band == 0, dst - 96 - src % 32, src % 32 - dst) >= 0
        parts = []
        for g in range(4):
            ones = jnp.where((src // 32 == g) & near, 1.0, 0.0).astype(BF16)
            parts.append(jnp.dot(halo_in[...], ones, preferred_element_type=F32))

        def scales(w):
            more = jnp.concatenate([part[w * 16 : w * 16 + 16] for part in parts], axis=0)
            return scale_of(SC[tile, w * CB : w * CB + CB, :] + more, w)

        turn(tile, scales)
        dy, dc = jnp.where(band == 1, tile - y + 4, y - tile + 4) % 4, (edge % 2) ^ core
        o = dy ^ (dy >> 1)
        n = place(o, dc)
        rows = W[pl.ds(pl.multiple_of((edge % 2) * 512 + late * 256, 256), 256), :]
        X[jnp.where(n == 0, 0, 72 + n), pl.ds(HALF * late, HALF)] = rows.astype(BF16).reshape(HALF, 16, 128)

        @pl.when(t != edge)
        def _():
            a2a_copy(n, late).start()

    def last_hop(src_slot, n, count, low, rows, target, row, sem):
        return pltpu.make_async_remote_copy(
            src_ref=X.at[pl.ds(src_slot * 8 + n, count), pl.ds(low, rows)],
            dst_ref=X4.at[pl.ds(n, count), pl.ds(low, rows)],
            send_sem=send.at[row, sem], recv_sem=recv.at[4, sem],
            device_id={"pair": target}, device_id_type=MESH,
        )

    def hop(src_slot, dst_slot, n, count, target, row, sem, recv_at):
        return pltpu.make_async_remote_copy(
            src_ref=X.at[pl.ds(src_slot * 8 + n, count)], dst_ref=X.at[pl.ds(dst_slot * 8 + n, count)],
            send_sem=send.at[row, sem], recv_sem=recv.at[dst_slot, recv_at],
            device_id={"pair": target}, device_id_type=MESH,
        )

    def half_hop(src_slot, dst_slot, n, h, target, row):
        rows = pl.ds(HALF * h, HALF)
        return pltpu.make_async_remote_copy(
            src_ref=X.at[src_slot * 8 + n, rows], dst_ref=X.at[dst_slot * 8 + n, rows],
            send_sem=send.at[row, 2 * n + h], recv_sem=recv.at[dst_slot, 2 * n + h],
            device_id={"pair": target}, device_id_type=MESH,
        )

    def first_forward(n, h):
        return half_hop(jnp.where(z == 7, 8, 0), 1, n, h, jnp.where(z == 7, far, nxt), 0)

    def exchange(n, h):
        return half_hop(0, 8, n, h, opp, 1)

    def first_back(n, h):
        return half_hop(jnp.where(z == 0, 0, 8), 7, n, h, jnp.where(z == 0, far, prv), 2)

    lag = jnp.where(t == edge, LAG, 0)
    early_half = jnp.where(t == edge, 1 - late, 0)

    def halves(n, do):
        @pl.when(n < 8)
        def _():
            do(n, early_half)

        @pl.when((n >= lag) & (n - lag < 8))
        def _():
            do(n - lag, 1 - early_half)

    def own_half(n, h):
        @pl.when(n > 0)
        def _():
            a2a_copy(n, h).wait_recv()

        exchange(n, h).start()

        @pl.when(z != 7)
        def _():
            first_forward(n, h).start()

        @pl.when(z == 0)
        def _():
            first_back(n, h).start()

    def opposite_half(n, h):
        exchange(n, h).wait_recv()

        @pl.when(z == 7)
        def _():
            first_forward(n, h).start()

        @pl.when(z != 0)
        def _():
            first_back(n, h).start()

    def pieces_in(copy, start, count=4):
        def one(n, c):
            for h in range(2):
                copy(n, h).wait_recv()
            return c

        lax.fori_loop(start, start + count, one, 0)

    def forward(slot, half):
        return hop(slot, slot + 1, 4 * half, 4, nxt, 2 + slot, half, half)

    def back(slot, quarter):
        return hop(slot, slot - 1, 2 * quarter, 2, prv, 13 - slot, quarter, quarter)

    def last_forward(part):
        if part == 0:
            return last_hop(3, 0, SPLIT, 0, FLO, nxt, 5, 0)
        return last_hop(3, SPLIT, 1, 0, CUT, nxt, 5, 1)

    def last_back(part):
        if part < 2:
            return last_hop(5, 4 + 2 * part, 2, 0, FLO, prv, 8, 2 + part)
        return last_hop(5, SPLIT, 1, CUT, FLO - CUT, prv, 8, 4)

    lane = iota((CB // 2, 128), 1)

    def prepare(fp, c):
        x = X[0:8, fp].reshape(128, 128).astype(F32)
        T[0:128, :] = x.T
        for hi in range(2):
            for odd in range(2):
                a = T[pl.ds(hi * 64 + odd, 32, stride=2), :]
                b = jnp.where(lane % 16 < 8, pltpu.roll(a, 120, 1), -pltpu.roll(a, 8, 1))
                LHS[hi * FLO + fp, 0:32, odd * 128 : odd * 128 + 128] = a.astype(BF16)
                LHS[hi * FLO + fp, 32:64, odd * 128 : odd * 128 + 128] = b.astype(BF16)
        return c

    def correlate(slot):
        place = slot - (slot > 4)
        products(
            lambda fp: X[pl.ds(slot * 8, 8), fp], LHS, O,
            lambda k: out.at[k, place],
        )

    whiten(0, 0)
    pl.semaphore_wait(barrier, jnp.where(wrap, 12, 11))
    halo = pltpu.make_async_remote_copy(
        src_ref=halo_out, dst_ref=halo_in, send_sem=halo_sem.at[0], recv_sem=halo_sem.at[1],
        device_id={"band": 1 - band}, device_id_type=MESH,
    )
    halo.start()
    give(1)
    halves(0, own_half)
    whiten(1, 0)
    give(2)
    whiten(2, 0)
    give(3)
    whiten(3, 0)

    @pl.when(t != edge)
    def _():
        halves(1, own_half)

    @pl.when(t == edge)
    def _():
        own_half(1, early_half)

    halo.wait_recv()
    whiten_edge()

    @pl.when(t == edge)
    def _():
        own_half(0, late)

    give(4)
    give(5)

    @pl.when(t == edge)
    def _():
        give(6)
        give(7)

    halves(0, opposite_half)

    def early(n, c):
        halves(n, own_half)

        @pl.when((n == 3) & (t != edge))
        def _():
            give(6)
            give(7)

        @pl.when(n == 8)
        def _():
            pieces_in(first_forward, 0)
            forward(1, 0).start()

        @pl.when(n > 2)
        def _():
            halves(n - 2, opposite_half)

        return c

    lax.fori_loop(2, 10 + LAG, early, 0)
    for quarter in (1, 2):
        pieces_in(first_back, 2 * quarter, 2)
        back(7, quarter).start()
    lax.fori_loop(0, FLO, prepare, 0)
    correlate(0)
    pieces_in(first_forward, 4)
    forward(1, 1).start()
    for quarter in (3, 0):
        pieces_in(first_back, 2 * quarter, 2)
        back(7, quarter).start()
    correlate(8)
    correlate(1)
    correlate(7)
    forward(1, 0).wait_recv()
    forward(2, 0).start()
    for quarter in (2, 3):
        back(7, quarter).wait_recv()
        back(6, quarter).start()
    forward(1, 1).wait_recv()
    forward(2, 1).start()
    correlate(2)
    for quarter in (0, 1):
        back(7, quarter).wait_recv()
        back(6, quarter).start()
    correlate(6)
    forward(2, 0).wait_recv()
    last_forward(0).start()
    last_forward(1).start()
    for part in range(2):
        back(6, 2 + part).wait_recv()
        last_back(part).start()
    forward(2, 1).wait_recv()
    correlate(3)
    for quarter in (0, 1):
        back(6, quarter).wait_recv()
    last_back(2).start()
    correlate(5)
    for part in range(2):
        last_forward(part).wait_recv()
    for part in range(3):
        last_back(part).wait_recv()
    halo.wait_send()

    def sent(n, c):
        for h in range(2):
            @pl.when(n > 0)
            def _():
                a2a_copy(n, h).wait_send()

            first_forward(n, h).wait_send()
            exchange(n, h).wait_send()
            first_back(n, h).wait_send()
        return c

    lax.fori_loop(0, 8, sent, 0)
    for half in range(2):
        for slot in (1, 2):
            forward(slot, half).wait_send()
    for quarter in range(4):
        for slot in (7, 6):
            back(slot, quarter).wait_send()
    for part in range(2):
        last_forward(part).wait_send()
    for part in range(3):
        last_back(part).wait_send()


def finish(part, LHS, X4, out, O, last, sem):
    copies = [
        pltpu.make_async_copy(part.at[k, s], out.at[k, s + (s > 3)], sem.at[k, s])
        for s in range(STEPS - 1) for k in range(2)
    ]
    for copy in copies:
        copy.start()
    products(lambda fp: X4[:, fp], LHS, O, lambda k: last.at[k])
    for k in range(2):
        copies.append(pltpu.make_async_copy(last.at[k], out.at[k, 4], sem.at[k, STEPS - 1]))
        copies[-1].start()
    for copy in copies:
        copy.wait()


def body(spectra, quality):
    in_vmem = pl.BlockSpec(memory_space=pltpu.VMEM)
    part, left, last = pl.pallas_call(
        kernel,
        out_shape=(
            jax.ShapeDtypeStruct((2, STEPS - 1, 64, CB * CB), BF16),
            jax.ShapeDtypeStruct((64, 64, 256), BF16),
            jax.ShapeDtypeStruct((PIECES, FLO, 16, 128), BF16),
        ),
        in_specs=[pl.BlockSpec(memory_space=pltpu.HBM)] * 2,
        out_specs=(in_vmem,) * 3,
        scratch_shapes=[
            pltpu.VMEM((2, WIN, CB, BAND), BF16),
            pltpu.VMEM((WIN, CB), jnp.int32),
            pltpu.VMEM((80, FLO, 16, 128), BF16),
            pltpu.VMEM((65 * PAD, 128), F32),
            pltpu.VMEM((4, WIN * CB, 128), F32),
            pltpu.VMEM((WIN * CB, BAND), BF16),
            pltpu.VMEM((WIN * CB, BAND), BF16),
            pltpu.VMEM((BAND, BAND), BF16),
            pltpu.VMEM((1056, 128), F32),
            pltpu.VMEM((136, 128), F32),
            pltpu.VMEM((128, 128), BF16),
            pltpu.VMEM((128, 128), BF16),
            pltpu.SemaphoreType.DMA((2,)),
            pltpu.SemaphoreType.DMA((2,)),
            pltpu.SemaphoreType.DMA((16,)),
            pltpu.SemaphoreType.DMA((9, 16)),
            pltpu.SemaphoreType.DMA((9, 16)),
        ],
        compiler_params=pltpu.CompilerParams(
            collective_id=0, has_side_effects=True, vmem_limit_bytes=LIMIT * 1024 * 1024
        ),
        cost_estimate=pl.CostEstimate(flops=1300000000, bytes_accessed=11000000, transcendentals=262144),
    )(*(pltpu.with_memory_space_constraint(x, pltpu.HBM) for x in (spectra, quality)))
    result = pl.pallas_call(
        finish,
        out_shape=jax.ShapeDtypeStruct((2, STEPS, 64, CB * CB), BF16),
        in_specs=[in_vmem] * 3,
        out_specs=pl.BlockSpec(memory_space=pl.ANY),
        scratch_shapes=[
            pltpu.VMEM((65 * PAD, 128), F32),
            pltpu.VMEM((2, 64, CB * CB), BF16),
            pltpu.SemaphoreType.DMA((2, STEPS)),
        ],
        compiler_params=pltpu.CompilerParams(vmem_limit_bytes=8 * 1024 * 1024),
    )(part, left, last)
    return result.reshape(1, 2, STEPS, 1, 64, CB * CB)


def solution(mesh):
    return jax.shard_map(
        body,
        mesh=mesh,
        in_specs=(P(None, "tm", "pair", "band"), P("tm", "pair")),
        out_specs=P("pair", None, None, "band", "tm", None),
        check_vma=False,
    )
```

```python
import jax
import jax.numpy as jnp
from jax import lax
from jax.experimental import pallas as pl
from jax.experimental.pallas import tpu as pltpu
from jax.sharding import PartitionSpec as P

MESH = pl.DeviceIdType.MESH
SMOOTH = 32
WIDTH = 2 * SMOOTH + 1
WIN = 8
CB = 64
BAND = 512
PIECES = 8
HALF = 16
FLO = 32
STEPS = 9
LAG = 1
LIMIT = 32
UNROLL = 8
SPLIT = 3
CUT = 24
PAD = 72
F32 = jnp.float32
BF16 = jnp.bfloat16


def iota(shape, dim):
    return lax.broadcasted_iota(jnp.int32, shape, dim)


def products(right, LHS, O, out):
    low64 = iota((128, 128), 1) < 64

    def some(g, c):
        for u in range(UNROLL):
            fp = g * UNROLL + u
            x = right(fp).reshape(128, 128).astype(F32)
            rolled = pltpu.roll(x, 64, 1)
            zero = jnp.zeros_like(x)
            r0 = jnp.concatenate([jnp.where(low64, x, zero), jnp.where(low64, zero, rolled)], axis=0).astype(BF16)
            r1 = jnp.concatenate([jnp.where(low64, rolled, zero), jnp.where(low64, zero, x)], axis=0).astype(BF16)
            for hi, r in ((0, r0), (1, r1)):
                f = fp + (fp // HALF + hi) * HALF
                O[pl.ds(f, 64, stride=PAD), :] = jnp.dot(LHS[hi * FLO + fp], r, preferred_element_type=F32)
        return c

    lax.fori_loop(0, FLO // UNROLL, some, 0)
    for k in range(2):
        for i in range(32):
            at = (k * 32 + i) * PAD
            out(k)[:, i * 128 : i * 128 + 128] = (O[at : at + 64, :] * 0.125).astype(BF16)


def kernel(
    spec_in, quality_in, out, LHS, X4,
    spec, quality, X, O, SC, PH, PL, BM, W, T, halo_out, halo_in,
    in_sem, halo_sem, a2a_send, recv, send,
):
    p = lax.axis_index("pair")
    t = lax.axis_index("tm")
    band = lax.axis_index("band")
    y, core = t // 2, t % 2
    nxt, prv, opp = (p + 1) % 16, (p + 15) % 16, (p + 8) % 16
    z = p % 8
    wrap = z % 7 == 0
    far = p - z + 7 - z
    load_spec = pltpu.make_async_copy(spec_in, spec, in_sem.at[0])
    load_quality = pltpu.make_async_copy(quality_in, quality, in_sem.at[1])
    load_spec.start()
    load_quality.start()

    barrier = pltpu.get_barrier_semaphore()
    for target in (nxt, prv, opp):
        pl.semaphore_signal(barrier, inc=1, device_id={"pair": target}, device_id_type=MESH)
    for step in range(1, 8):
        pl.semaphore_signal(barrier, inc=1, device_id={"tm": (t + step) % 8}, device_id_type=MESH)
    pl.semaphore_signal(barrier, inc=1, device_id={"band": 1 - band}, device_id_type=MESH)

    @pl.when(wrap)
    def _():
        pl.semaphore_signal(barrier, inc=1, device_id={"pair": far}, device_id_type=MESH)

    BM[...] = jnp.where(jnp.abs(iota((BAND, BAND), 0) - iota((BAND, BAND), 1)) <= SMOOTH, 1.0, 0.0).astype(BF16)
    load_spec.wait()
    load_quality.wait()

    def power(w, lanes):
        re = spec[0, w, :, lanes].astype(F32)
        im = spec[1, w, :, lanes].astype(F32)
        return re * re + im * im

    group = iota((16, 128), 1) // 32
    for w in range(WIN):
        last = pltpu.roll(power(w, slice(BAND - 128, BAND)), 32, 1)
        first = power(w, slice(0, 128))
        edge = jnp.where(band == 0, last, first)
        packed = edge[0:16]
        for g in range(1, 4):
            packed = jnp.where(group == g, pltpu.roll(edge[16 * g : 16 * g + 16], 32 * g, 1), packed)
        halo_out[w * 16 : w * 16 + 16, :] = packed.astype(BF16)

    def split(w, c):
        pw = power(w, slice(None))
        hi = pw.astype(BF16)
        rows = pl.ds(pl.multiple_of(w * CB, CB), CB)
        PH[rows, :] = hi
        PL[rows, :] = (pw - hi.astype(F32)).astype(BF16)
        return c

    lax.fori_loop(0, WIN, split, 0)

    def smooth(m, c):
        rows = pl.ds(pl.multiple_of(m * 128, 128), 128)
        total = jnp.dot(PH[rows, :], BM[...], preferred_element_type=F32)
        total += jnp.dot(PL[rows, :], BM[...], preferred_element_type=F32)
        for tile in range(4):
            SC[tile, rows, :] = total[:, tile * 128 : tile * 128 + 128]
        return c

    lax.fori_loop(0, WIN * CB // 128, smooth, 0)

    eye = iota((CB, CB), 0) == iota((CB, CB), 1)

    def column(w):
        return jnp.sum(jnp.where(eye, quality[w : w + 1, :].astype(F32), 0.0), axis=1, keepdims=True)

    def scale_of(total, w):
        return lax.rsqrt(total * (1.0 / WIDTH) + 1e-06) * column(w)

    def chip(o):
        dy = o ^ (o >> 1)
        return jnp.where(band == 1, y + dy, y - dy + 4) % 4

    def place(o, dc):
        return jnp.where(o == 0, dc, jnp.where(o == 3, 6 + dc, 1 + o + 2 * dc))

    def a2a_target(n):
        o = jnp.where(n < 2, 0, jnp.where(n < 6, 1 + n % 2, 3))
        dc = jnp.where(n < 2, n, jnp.where(n < 4, 0, jnp.where(n < 6, 1, n - 6)))
        return 2 * chip(o) + (core ^ dc)

    def a2a_copy(n, h):
        rows = pl.ds(HALF * h, HALF)
        return pltpu.make_async_remote_copy(
            src_ref=X.at[72 + n, rows], dst_ref=X.at[n, rows], send_sem=a2a_send.at[2 * n + h], recv_sem=recv.at[0, 2 * n + h],
            device_id={"tm": a2a_target(n)}, device_id_type=MESH,
        )

    low = iota((CB, 128), 1) % 32 < 16

    def turn(tile, scales):
        lanes = pl.ds(pl.multiple_of(tile * 128, 128), 128)
        for w in range(WIN):
            scale = scales(w)
            re = spec[0, w, :, lanes].astype(F32) * scale
            im = spec[1, w, :, lanes].astype(F32) * scale
            top = jnp.where(low, re, pltpu.roll(im, 16, 1))
            bottom = jnp.where(low, pltpu.roll(re, 112, 1), im)
            turned = jnp.concatenate([top, bottom], axis=0).T
            for half in range(2):
                for h in range(2):
                    for k in range(2):
                        at = half * 64 + h * 32 + k * 16
                        W[pl.ds(half * 512 + h * 256 + k * 8 + w, HALF, stride=16), :] = turned[at : at + 16]

    def keep(o, dc, rows):
        n = place(o, dc)
        X[jnp.where(n == 0, 0, 72 + n)] = rows.astype(BF16).reshape(FLO, 16, 128)

    edge = jnp.where(band == 0, 7, 0)
    late = 1 - band

    def whiten(o, c):
        tile = chip(o)
        turn(tile, lambda w: scale_of(SC[tile, w * CB : w * CB + CB, :], w))
        for half in range(2):
            keep(o, half ^ core, W[half * 512 : half * 512 + 512, :])
        return c

    def give(n):
        for h in range(2):
            @pl.when((a2a_target(n) != edge) | (late != h))
            def _():
                a2a_copy(n, h).start()

    def whiten_edge():
        src, dst = iota((128, 128), 0), iota((128, 128), 1)
        tile = edge // 2
        near = jnp.where(band == 0, dst - 96 - src % 32, src % 32 - dst) >= 0
        parts = []
        for g in range(4):
            ones = jnp.where((src // 32 == g) & near, 1.0, 0.0).astype(BF16)
            parts.append(jnp.dot(halo_in[...], ones, preferred_element_type=F32))

        def scales(w):
            more = jnp.concatenate([part[w * 16 : w * 16 + 16] for part in parts], axis=0)
            return scale_of(SC[tile, w * CB : w * CB + CB, :] + more, w)

        turn(tile, scales)
        dy, dc = jnp.where(band == 1, tile - y + 4, y - tile + 4) % 4, (edge % 2) ^ core
        o = dy ^ (dy >> 1)
        n = place(o, dc)
        rows = W[pl.ds(pl.multiple_of((edge % 2) * 512 + late * 256, 256), 256), :]
        X[jnp.where(n == 0, 0, 72 + n), pl.ds(HALF * late, HALF)] = rows.astype(BF16).reshape(HALF, 16, 128)

        @pl.when(t != edge)
        def _():
            a2a_copy(n, late).start()

    def last_hop(src_slot, n, count, low, rows, target, row, sem):
        return pltpu.make_async_remote_copy(
            src_ref=X.at[pl.ds(src_slot * 8 + n, count), pl.ds(low, rows)],
            dst_ref=X4.at[pl.ds(n, count), pl.ds(low, rows)],
            send_sem=send.at[row, sem], recv_sem=recv.at[4, sem],
            device_id={"pair": target}, device_id_type=MESH,
        )

    def hop(src_slot, dst_slot, n, count, target, row, sem, recv_at):
        return pltpu.make_async_remote_copy(
            src_ref=X.at[pl.ds(src_slot * 8 + n, count)], dst_ref=X.at[pl.ds(dst_slot * 8 + n, count)],
            send_sem=send.at[row, sem], recv_sem=recv.at[dst_slot, recv_at],
            device_id={"pair": target}, device_id_type=MESH,
        )

    def half_hop(src_slot, dst_slot, n, h, target, row):
        rows = pl.ds(HALF * h, HALF)
        return pltpu.make_async_remote_copy(
            src_ref=X.at[src_slot * 8 + n, rows], dst_ref=X.at[dst_slot * 8 + n, rows],
            send_sem=send.at[row, 2 * n + h], recv_sem=recv.at[dst_slot, 2 * n + h],
            device_id={"pair": target}, device_id_type=MESH,
        )

    def first_forward(n, h):
        return half_hop(jnp.where(z == 7, 8, 0), 1, n, h, jnp.where(z == 7, far, nxt), 0)

    def exchange(n, h):
        return half_hop(0, 8, n, h, opp, 1)

    def first_back(n, h):
        return half_hop(jnp.where(z == 0, 0, 8), 7, n, h, jnp.where(z == 0, far, prv), 2)

    lag = jnp.where(t == edge, LAG, 0)
    early_half = jnp.where(t == edge, 1 - late, 0)

    def halves(n, do):
        @pl.when(n < 8)
        def _():
            do(n, early_half)

        @pl.when((n >= lag) & (n - lag < 8))
        def _():
            do(n - lag, 1 - early_half)

    def own_half(n, h):
        @pl.when(n > 0)
        def _():
            a2a_copy(n, h).wait_recv()

        exchange(n, h).start()

        @pl.when(z != 7)
        def _():
            first_forward(n, h).start()

        @pl.when(z == 0)
        def _():
            first_back(n, h).start()

    def opposite_half(n, h):
        exchange(n, h).wait_recv()

        @pl.when(z == 7)
        def _():
            first_forward(n, h).start()

        @pl.when(z != 0)
        def _():
            first_back(n, h).start()

    def pieces_in(copy, start, count=4):
        def one(n, c):
            for h in range(2):
                copy(n, h).wait_recv()
            return c

        lax.fori_loop(start, start + count, one, 0)

    def forward(slot, half):
        return hop(slot, slot + 1, 4 * half, 4, nxt, 2 + slot, half, half)

    def back(slot, quarter):
        return hop(slot, slot - 1, 2 * quarter, 2, prv, 13 - slot, quarter, quarter)

    def last_forward(part):
        if part == 0:
            return last_hop(3, 0, SPLIT, 0, FLO, nxt, 5, 0)
        return last_hop(3, SPLIT, 1, 0, CUT, nxt, 5, 1)

    def last_back(part):
        if part < 2:
            return last_hop(5, 4 + 2 * part, 2, 0, FLO, prv, 8, 2 + part)
        return last_hop(5, SPLIT, 1, CUT, FLO - CUT, prv, 8, 4)

    lane = iota((CB // 2, 128), 1)

    def prepare(fp, c):
        x = X[0:8, fp].reshape(128, 128).astype(F32)
        T[0:128, :] = x.T
        for hi in range(2):
            for odd in range(2):
                a = T[pl.ds(hi * 64 + odd, 32, stride=2), :]
                b = jnp.where(lane % 16 < 8, pltpu.roll(a, 120, 1), -pltpu.roll(a, 8, 1))
                LHS[hi * FLO + fp, 0:32, odd * 128 : odd * 128 + 128] = a.astype(BF16)
                LHS[hi * FLO + fp, 32:64, odd * 128 : odd * 128 + 128] = b.astype(BF16)
        return c

    def correlate(slot):
        place = slot - (slot > 4)
        products(
            lambda fp: X[pl.ds(slot * 8, 8), fp], LHS, O,
            lambda k: out.at[k, place],
        )

    whiten(0, 0)
    pl.semaphore_wait(barrier, jnp.where(wrap, 12, 11))
    halo = pltpu.make_async_remote_copy(
        src_ref=halo_out, dst_ref=halo_in, send_sem=halo_sem.at[0], recv_sem=halo_sem.at[1],
        device_id={"band": 1 - band}, device_id_type=MESH,
    )
    halo.start()
    give(1)
    halves(0, own_half)
    whiten(1, 0)
    give(2)
    whiten(2, 0)
    give(3)
    whiten(3, 0)

    @pl.when(t != edge)
    def _():
        halves(1, own_half)

    @pl.when(t == edge)
    def _():
        own_half(1, early_half)

    halo.wait_recv()
    whiten_edge()

    @pl.when(t == edge)
    def _():
        own_half(0, late)

    give(4)
    give(5)

    @pl.when(t == edge)
    def _():
        give(6)
        give(7)

    halves(0, opposite_half)

    def early(n, c):
        halves(n, own_half)

        @pl.when((n == 3) & (t != edge))
        def _():
            give(6)
            give(7)

        @pl.when(n == 8)
        def _():
            pieces_in(first_forward, 0)
            forward(1, 0).start()

        @pl.when(n > 2)
        def _():
            halves(n - 2, opposite_half)

        return c

    lax.fori_loop(2, 10 + LAG, early, 0)
    for quarter in (1, 2):
        pieces_in(first_back, 2 * quarter, 2)
        back(7, quarter).start()
    lax.fori_loop(0, FLO, prepare, 0)
    correlate(0)
    pieces_in(first_forward, 4)
    forward(1, 1).start()
    for quarter in (3, 0):
        pieces_in(first_back, 2 * quarter, 2)
        back(7, quarter).start()
    correlate(8)
    correlate(1)
    correlate(7)
    forward(1, 0).wait_recv()
    forward(2, 0).start()
    for quarter in (2, 3):
        back(7, quarter).wait_recv()
        back(6, quarter).start()
    forward(1, 1).wait_recv()
    forward(2, 1).start()
    correlate(2)
    for quarter in (0, 1):
        back(7, quarter).wait_recv()
        back(6, quarter).start()
    correlate(6)
    forward(2, 0).wait_recv()
    last_forward(0).start()
    last_forward(1).start()
    for part in range(2):
        back(6, 2 + part).wait_recv()
        last_back(part).start()
    forward(2, 1).wait_recv()
    correlate(3)
    for quarter in (0, 1):
        back(6, quarter).wait_recv()
    last_back(2).start()
    correlate(5)
    halo.wait_send()

    def sent(n, c):
        for h in range(2):
            @pl.when(n > 0)
            def _():
                a2a_copy(n, h).wait_send()

            first_forward(n, h).wait_send()
            exchange(n, h).wait_send()
            first_back(n, h).wait_send()
        return c

    lax.fori_loop(0, 8, sent, 0)
    for half in range(2):
        for slot in (1, 2):
            forward(slot, half).wait_send()
    for quarter in range(4):
        for slot in (7, 6):
            back(slot, quarter).wait_send()
    for part in range(2):
        last_forward(part).wait_recv()
    for part in range(3):
        last_back(part).wait_recv()
    for part in range(2):
        last_forward(part).wait_send()
    for part in range(3):
        last_back(part).wait_send()


def finish(part, LHS, X4, out, O, last, sem):
    copies = [
        pltpu.make_async_copy(part.at[k, s], out.at[k, s + (s > 3)], sem.at[k, s])
        for s in range(STEPS - 1) for k in range(2)
    ]
    for copy in copies:
        copy.start()
    products(lambda fp: X4[:, fp], LHS, O, lambda k: last.at[k])
    for k in range(2):
        copies.append(pltpu.make_async_copy(last.at[k], out.at[k, 4], sem.at[k, STEPS - 1]))
        copies[-1].start()
    for copy in copies:
        copy.wait()


def body(spectra, quality):
    in_vmem = pl.BlockSpec(memory_space=pltpu.VMEM)
    part, left, last = pl.pallas_call(
        kernel,
        out_shape=(
            jax.ShapeDtypeStruct((2, STEPS - 1, 64, CB * CB), BF16),
            jax.ShapeDtypeStruct((64, 64, 256), BF16),
            jax.ShapeDtypeStruct((PIECES, FLO, 16, 128), BF16),
        ),
        in_specs=[pl.BlockSpec(memory_space=pltpu.HBM)] * 2,
        out_specs=(in_vmem,) * 3,
        scratch_shapes=[
            pltpu.VMEM((2, WIN, CB, BAND), BF16),
            pltpu.VMEM((WIN, CB), jnp.int32),
            pltpu.VMEM((80, FLO, 16, 128), BF16),
            pltpu.VMEM((65 * PAD, 128), F32),
            pltpu.VMEM((4, WIN * CB, 128), F32),
            pltpu.VMEM((WIN * CB, BAND), BF16),
            pltpu.VMEM((WIN * CB, BAND), BF16),
            pltpu.VMEM((BAND, BAND), BF16),
            pltpu.VMEM((1056, 128), F32),
            pltpu.VMEM((136, 128), F32),
            pltpu.VMEM((128, 128), BF16),
            pltpu.VMEM((128, 128), BF16),
            pltpu.SemaphoreType.DMA((2,)),
            pltpu.SemaphoreType.DMA((2,)),
            pltpu.SemaphoreType.DMA((16,)),
            pltpu.SemaphoreType.DMA((9, 16)),
            pltpu.SemaphoreType.DMA((9, 16)),
        ],
        compiler_params=pltpu.CompilerParams(
            collective_id=0, has_side_effects=True, vmem_limit_bytes=LIMIT * 1024 * 1024
        ),
        cost_estimate=pl.CostEstimate(flops=1300000000, bytes_accessed=11000000, transcendentals=262144),
    )(*(pltpu.with_memory_space_constraint(x, pltpu.HBM) for x in (spectra, quality)))
    result = pl.pallas_call(
        finish,
        out_shape=jax.ShapeDtypeStruct((2, STEPS, 64, CB * CB), BF16),
        in_specs=[in_vmem] * 3,
        out_specs=pl.BlockSpec(memory_space=pl.ANY),
        scratch_shapes=[
            pltpu.VMEM((65 * PAD, 128), F32),
            pltpu.VMEM((2, 64, CB * CB), BF16),
            pltpu.SemaphoreType.DMA((2, STEPS)),
        ],
        compiler_params=pltpu.CompilerParams(vmem_limit_bytes=8 * 1024 * 1024),
    )(part, left, last)
    return result.reshape(1, 2, STEPS, 1, 64, CB * CB)


def solution(mesh):
    return jax.shard_map(
        body,
        mesh=mesh,
        in_specs=(P(None, "tm", "pair", "band"), P("tm", "pair")),
        out_specs=P("pair", None, None, "band", "tm", None),
        check_vma=False,
    )
```
